768 devices in a mesh: slab: 192 (over y, z, core), col: 4 (over x).
Axes of the slice: x: 4, y: 8, z: 12, core: 2. Of those that a mesh axis runs over, the one named last changes fastest.
Arguments:
- prolong: bfloat16 [384, 8, 6, 4096], P('slab', 'col'), may hold values from -1 to 1
- coupling: bfloat16 [384, 8, 6, 28672], P('slab', 'col'), may hold values from -0.75 to 0.75
- jacobi_scale: bfloat16 [384, 8, 6, 64], P('slab', 'col'), may hold values from 0.19921875 to 0.59765625
- owner: int32 [2304, 1], P(('slab', 'col')), may hold values from 0 to 3; in each aligned block of 3 rows (0 to 2, 3 to 5, ...) at most 2 rows name the same one
Outputs:
- coarse_rows: bfloat16 [6144, 64, 448], P(('slab', 'col'))
The draws below stay inside these ranges and needn't reach their ends.
Inputs may be any that keep to these rules, and one draw needn't show every extreme that they name: Each device's 3 rows name every owner at most 2 times, and in some devices one owner exactly 2 times.
All inputs are finite; a program needn't handle non-finite values.
Results may differ from the reference program's by a relative error of at most 0.0061.
Values may be sent and summed in bfloat16 or wider, within the bound.
No kernel may reach another device: no remote copies, remote signals or barrier semaphores. Data moves between devices by JAX's collectives and lax.ppermute only.
A program may use at most 32 MiB of HBM per device.

```python
import math
import jax
import jax.numpy as jnp
import numpy as np
from jax import lax

FD = 64
KC = 64
SX = 6
SY = 2
SZ = 2
AGG_DEV = 3
CAPS = 2
SLOTS = 8
NY = 8
NZ = 384
NAGG = 2304
TOTAL_SLOTS = 6144
N_SLAB = 192
N_COL = 4


def steps_of(stream_key, extent, pieces, least, largest):
    level, own = 1.0, jax.random.fold_in(stream_key, 6)
    for dim, shards_of in pieces:
        draws = jnp.exp(jax.random.uniform(jax.random.fold_in(own, dim), (shards_of,), jnp.float32, least / len(pieces), largest / len(pieces)))
        level = level * jnp.repeat(draws, extent[dim] // shards_of).reshape([-1 if axis == dim else 1 for axis in range(len(extent))])
    return level


def assign_block(stream_key, own, number, rows, number_of, top, bound, lean):
    sequence = jax.random.permutation(stream_key, number_of)
    heavy_load, usual = portions_of(number_of, rows * top, bound, lean, True), portions_of(number_of, rows * top, bound, lean, False)
    places = jnp.arange(number_of)

    def named(sizes, turn):
        used = int((sizes > 0).sum())
        fixed = max(1, used // 4)
        shifted = fixed + (places - fixed + turn * (used - fixed)) % max(1, number_of - fixed)
        return jnp.zeros((number_of,), jnp.int32).at[sequence[jnp.where(places < fixed, places, shifted)]].set(jnp.asarray(sizes, jnp.int32))

    sizes = jnp.where(number % 4 == 0, named(heavy_load, number // 4), named(usual, number - number // 4 - 1))
    mixed = jax.random.permutation(jax.random.fold_in(own, 3), number_of)
    donor, sink = mixed[0:number_of // 2 * 2:2], mixed[1:number_of // 2 * 2:2]
    room = jnp.minimum(sizes[donor] - 1, bound - sizes[sink]) // 2
    room = jnp.where((donor == sequence[0]) | (sink == sequence[0]) | (sizes[sink] == 0), 0, jnp.maximum(room, 0))
    shifted = jax.random.randint(jax.random.fold_in(own, 4), (number_of // 2,), 0, 1 << 20) % (room + 1)
    sizes = sizes.at[donor].add(-shifted).at[sink].add(shifted)
    labels = jnp.searchsorted(jnp.cumsum(sizes), jnp.arange(rows * top), side="right").astype(jnp.int32)
    grid = labels.reshape(top, rows).T
    grid = grid[jax.random.permutation(jax.random.fold_in(own, 1), rows)]
    turn = jax.random.randint(jax.random.fold_in(own, 2), (rows, 1), 0, top)
    return jnp.take_along_axis(grid, (jnp.arange(top)[None, :] + turn) % top, axis=1)


def portions_of(amount, total, bound, slope, full):
    weights = [(1 << 20) // math.isqrt(standing ** slope) + 1 for standing in range(1, amount + 1)]
    largest = bound if full else min(bound, max(-(-total // amount), total * weights[0] // sum(weights)))
    least = 1 if total - largest >= amount - 1 else 0
    holding, rest = [largest] + [least] * (amount - 1), total - largest - least * (amount - 1)
    while rest > 0:
        free = [i for i in range(1, amount) if holding[i] < largest] or [i for i in range(1, amount) if holding[i] < bound]
        pool, left = sum([weights[i] for i in free]), rest
        for i in free:
            extra = min(bound - holding[i], max(1, left * weights[i] // pool), rest)
            holding[i] = holding[i] + extra
            rest = rest - extra
    return np.array(holding)


def normal_values(own_key, dims, scale, most, pieces=(), held_as=jnp.bfloat16):
    array = scale * jax.random.normal(own_key, dims, jnp.float32)
    if pieces:
        array = array * steps_of(own_key, dims, pieces, -0.22, 0.18)
    return jnp.clip(array, -most, most).astype(held_as)


def setup_inputs(seed: int = 0) -> dict:
    splits = jax.random.split(jax.random.key(seed), 5)
    prolong = normal_values(splits[0], (NZ, NY, SX, FD * KC), 0.125, 1.0, ((0, 192), (1, 4)))
    coupling = normal_values(splits[1], (NZ, NY, SX, 7 * FD * FD), FD ** -0.5, 0.75, ((0, 192), (1, 4)))
    jacobi_scale = jnp.clip(jnp.exp(math.log(0.59765625) - 1.0986123 * jax.random.uniform(splits[2], (NZ, NY, SX, FD), jnp.float32) ** steps_of(splits[2], (NZ, NY, SX, FD), ((0, 192), (1, 4)), -0.2, 0.2)), 0.19921875, 0.59765625).astype(jnp.bfloat16)
    owner_keys = jax.random.split(jax.random.fold_in(splits[3], 1), NAGG // AGG_DEV)
    owner_turns = jax.random.permutation(jax.random.fold_in(splits[3], 3), NAGG // AGG_DEV)
    owner = jax.vmap(lambda own, number: assign_block(jax.random.fold_in(splits[3], 2), own, number, AGG_DEV, N_COL, 1, CAPS, 2))(owner_keys, owner_turns).reshape((NAGG, 1))
    return dict(prolong=prolong, coupling=coupling, jacobi_scale=jacobi_scale, owner=owner)


OFFSETS = ((1, 1, 1), (1, 1, 0), (1, 1, 2), (1, 0, 1), (1, 2, 1), (0, 1, 1), (2, 1, 1))


def smooth(tentative, self_block, scaling):
    product = jnp.einsum('yxij,yxjk->yxik', self_block.astype(jnp.float32), tentative.astype(jnp.float32))
    return (tentative.astype(jnp.float32) - scaling.astype(jnp.float32)[..., None] * product).astype(jnp.bfloat16)


def coarse_blocks(padded, blocks):
    layers, across, length = blocks.shape[0], blocks.shape[1], blocks.shape[2]
    own = padded[1:-1, 1:-1, 1:-1].astype(jnp.float32)
    coords = (lax.broadcasted_iota(jnp.int32, (layers, across, length), 2),
              lax.broadcasted_iota(jnp.int32, (layers, across, length), 1),
              lax.broadcasted_iota(jnp.int32, (layers, across, length), 0))
    parts = []
    total_self = jnp.zeros((layers, across, length, KC, KC), jnp.float32)
    for direction in range(7):
        off_z, off_y, off_x = OFFSETS[direction]
        neighbor = padded[off_z:off_z + layers, off_y:off_y + across, off_x:off_x + length].astype(jnp.float32)
        left = jnp.einsum('zyxik,zyxij->zyxkj', own, blocks[:, :, :, direction].astype(jnp.float32)).astype(jnp.bfloat16)
        term = jnp.einsum('zyxkj,zyxjl->zyxkl', left.astype(jnp.float32), neighbor)
        if direction == 0:
            total_self = total_self + term
        else:
            inside = (coords[(direction - 1) // 2] % 2 == direction % 2).astype(jnp.float32)[..., None, None]
            total_self = total_self + inside * term
            parts.append((1.0 - inside) * term)
    stacked = jnp.stack([total_self] + parts, axis=4)
    summed = stacked.reshape(layers // 2, 2, across // 2, 2, length // 2, 2, KC, 7, KC).sum(axis=(1, 3, 5))
    return summed.reshape(layers // 2, across // 2, length // 2, KC, 7 * KC).astype(jnp.bfloat16)


def reference(prolong, coupling, jacobi_scale, owner):
    tentative = prolong.reshape(NZ, NY, SX, FD, KC)
    blocks = coupling.reshape(NZ, NY, SX, 7, FD, FD)
    smoothed = lax.map(lambda item: smooth(item[0], item[1][:, :, 0], item[2]), (tentative, blocks, jacobi_scale))
    padded = jnp.pad(smoothed, ((1, 1), (1, 1), (1, 1), (0, 0), (0, 0)))

    def one_pair(pair_index):
        start = (2 * pair_index).astype(jnp.int32)
        window = lax.dynamic_slice_in_dim(padded, start, 4, 0)
        layer_blocks = lax.dynamic_slice_in_dim(blocks, start, 2, 0)
        return coarse_blocks(window, layer_blocks)[0]

    rows = lax.map(one_pair, jnp.arange(NZ // 2, dtype=jnp.int32))
    rows = rows.reshape(N_SLAB, SZ // 2, N_COL, SY // 2, SX // 2, KC, 7 * KC)
    rows = jnp.transpose(rows, (0, 2, 1, 3, 4, 5, 6)).reshape(NAGG, KC, 7 * KC)
    devices_all = N_SLAB * N_COL
    target = owner[:, 0].reshape(devices_all, AGG_DEV)
    hits = (target[:, :, None] == jnp.arange(N_COL, dtype=jnp.int32)[None, None, :]).astype(jnp.int32)
    rank = jnp.sum((jnp.cumsum(hits, axis=1) - hits) * hits, axis=2)
    device_ids = jnp.arange(devices_all, dtype=jnp.int32)[:, None]
    slab_ids = device_ids // N_COL
    col_ids = device_ids % N_COL
    destination = (slab_ids * N_COL + target) * SLOTS + col_ids * CAPS + rank
    result = jnp.zeros((TOTAL_SLOTS, KC, 7 * KC), jnp.bfloat16)
    return result.at[destination.reshape(-1)].set(rows)
```

```python
import functools

import jax
import jax.numpy as jnp
from jax import lax
from jax.experimental import pallas as pl
from jax.experimental.pallas import tpu as pltpu
from jax.sharding import PartitionSpec as P

FD = 64
LX = 6
LZ = 2
F32 = jnp.float32
BF16 = jnp.bfloat16


def low_lanes(rows):
    return lax.broadcasted_iota(jnp.int32, (rows, 128), 1) < 64


def even_rows(rows):
    return lax.broadcasted_iota(jnp.int32, (rows, 128), 0) % 2 == 0


def swap_halves(block):
    return jnp.concatenate([block[:, 64:], block[:, :64]], axis=1)


def unpairing():
    row = lax.broadcasted_iota(jnp.int32, (128, 128), 0)
    col = lax.broadcasted_iota(jnp.int32, (128, 128), 1)
    same_y = row // 64 == col % 2
    same_i = row % 64 == (col % 64) // 2 * 2 + col // 64
    return (same_y & same_i).astype(F32).astype(BF16)


def doubled(paired, matrix):
    swapped = swap_halves(paired)
    low = low_lanes(64)
    stacked = jnp.concatenate([jnp.where(low, paired, swapped), jnp.where(low, swapped, paired)], axis=0)
    return jnp.dot(matrix, stacked, preferred_element_type=F32).astype(BF16)


def diagonal(twice):
    low = low_lanes(64)
    zero = jnp.zeros_like(twice)
    return jnp.concatenate([jnp.where(low, twice, zero), jnp.where(low, zero, twice)], axis=0)


def diagonal_of_packed(packed):
    low = low_lanes(32)
    swapped = swap_halves(packed)
    zero = jnp.zeros_like(packed)
    return jnp.concatenate(
        [
            jnp.where(low, packed, zero),
            jnp.where(low, swapped, zero),
            jnp.where(low, zero, swapped),
            jnp.where(low, zero, packed),
        ],
        axis=0,
    )


def pick_y(both):
    return jnp.where(even_rows(64), both[:, :128], both[:, 128:])


def smooth_kernel(p_ref, c_ref, s_ref, smooth_ref, twice_ref, zlo_ref, zhi_ref, ylo_ref, yhi_ref):
    pairs = LZ * LX
    rows = pairs * 64
    matrix = unpairing()
    row = lax.broadcasted_iota(jnp.int32, (rows, 2 * pairs), 0)
    col = lax.broadcasted_iota(jnp.int32, (rows, 2 * pairs), 1)
    picks = (col == row // 64 * 2 + row % 2).astype(F32).astype(BF16)
    spread = jnp.dot(picks, s_ref[...], preferred_element_type=F32)
    row = lax.broadcasted_iota(jnp.int32, (rows, 64), 0)
    col = lax.broadcasted_iota(jnp.int32, (rows, 64), 1)
    spread = jnp.where(row % 64 // 2 == col // 2, spread, 0.0).astype(BF16)
    row = lax.broadcasted_iota(jnp.int32, (64, 128), 0)
    col = lax.broadcasted_iota(jnp.int32, (64, 128), 1)
    halves = (row % 2 == col // 64).astype(F32).astype(BF16)
    scale = jnp.dot(spread, halves, preferred_element_type=F32)
    low = low_lanes(32)
    for z in range(LZ):
        for x in range(LX):
            n = z * LX + x
            tentative = p_ref[n * 64 : n * 64 + 64, :]
            twice = doubled(tentative, matrix)
            right = jnp.concatenate([diagonal(twice[:64]), diagonal(twice[64:])], axis=1)
            both = jnp.dot(c_ref[n, :64, :], right, preferred_element_type=F32)
            smoothed = (tentative.astype(F32) - scale[n * 64 : n * 64 + 64] * pick_y(both)).astype(BF16)
            smooth_ref[n * 64 : n * 64 + 64, :] = smoothed
            twice = doubled(smoothed, matrix)
            twice_ref[n] = twice
            for y in range(2):
                packed = jnp.where(low, twice[y * 64 : y * 64 + 32], twice[y * 64 + 32 : y * 64 + 64])
                at = (x * 2 + y) * 32
                (zlo_ref, zhi_ref)[z][at : at + 32, :] = packed
                at = n * 32
                (ylo_ref, yhi_ref)[y][at : at + 32, :] = packed


def combine(even, odd):
    low = low_lanes(64)
    return jnp.where(low, even[:64], odd[64:]) + swap_halves(jnp.where(low, odd[:64], even[64:]))


def transposed_dot(left, right):
    return lax.dot_general(left, right, (((0,), (0,)), ((), ())), preferred_element_type=F32)


def local_kernel(c_ref, smooth_ref, twice_ref, part_ref):
    def both_y(n, swapped=False):
        twice = twice_ref[n]
        first, second = diagonal(twice[:64]), diagonal(twice[64:])
        return jnp.concatenate([second, first] if swapped else [first, second], axis=1)

    even = even_rows(64)
    inner, outer = {}, {}
    for z in range(LZ):
        for x in range(LX):
            n = z * LX + x
            block = lambda d: c_ref[n, d * 64 : d * 64 + 64, :]
            across = jnp.where(even, block(4), block(3))
            left = jnp.concatenate([block(0), block(2 - x % 2), block(6 - z), across], axis=1)
            right = jnp.concatenate(
                [both_y(n), both_y(z * LX + (x ^ 1)), both_y((1 - z) * LX + x), both_y(n, True)], axis=0
            )
            inner[z, x] = pick_y(jnp.dot(left, right, preferred_element_type=F32)).astype(BF16)
            beside = x - 1 if x % 2 == 0 else x + 1
            if 0 <= beside < LX:
                outer[z, x] = pick_y(
                    jnp.dot(block(1 + x % 2), both_y(z * LX + beside), preferred_element_type=F32)
                ).astype(BF16)
    for a in range(LX // 2):
        own = {}
        for z in range(LZ):
            for x in (2 * a, 2 * a + 1):
                n = z * LX + x
                own[z, x] = smooth_ref[n * 64 : n * 64 + 64, :]
        order = [(z, x) for z in range(LZ) for x in (2 * a, 2 * a + 1)]
        total = transposed_dot(
            jnp.concatenate([own[k] for k in order], axis=0), jnp.concatenate([inner[k] for k in order], axis=0)
        )
        sides = []
        for x in (2 * a, 2 * a + 1):
            if (0, x) in outer:
                sides.append(
                    transposed_dot(
                        jnp.concatenate([own[0, x], own[1, x]], axis=0),
                        jnp.concatenate([outer[0, x], outer[1, x]], axis=0),
                    )
                )
            else:
                sides.append(jnp.zeros((128, 128), F32))
        part_ref[a, :, :128] = combine(total, sides[0]).astype(BF16)
        part_ref[a, :, 128:] = combine(sides[1], jnp.zeros((128, 128), F32)).astype(BF16)


def halo_kernel(owner_ref, c_ref, smooth_ref, part_ref, zlo_ref, zhi_ref, ylo_ref, yhi_ref, out_ref):
    even = even_rows(64)
    across, along = {}, {}
    for z in range(LZ):
        for x in range(LX):
            n = z * LX + x
            block = lambda d: c_ref[n, d * 64 : d * 64 + 64, :]
            right = jnp.concatenate(
                [diagonal_of_packed(ref[n * 32 : n * 32 + 32, :]) for ref in (ylo_ref, yhi_ref)], axis=1
            )
            left = jnp.where(even, block(3), block(4))
            across[z, x] = pick_y(jnp.dot(left, right, preferred_element_type=F32)).astype(BF16)
            ref = (zlo_ref, zhi_ref)[z]
            right = jnp.concatenate(
                [diagonal_of_packed(ref[(x * 2 + y) * 32 : (x * 2 + y) * 32 + 32, :]) for y in range(2)], axis=1
            )
            along[z, x] = pick_y(jnp.dot(block(5 + z), right, preferred_element_type=F32)).astype(BF16)
    out_ref[...] = jnp.zeros_like(out_ref)
    zero = jnp.zeros((64, 128), BF16)
    low = low_lanes(64)
    owners = [owner_ref[a, 0] for a in range(LX // 2)]
    for a in range(LX // 2):
        own = {}
        for z in range(LZ):
            for x in (2 * a, 2 * a + 1):
                n = z * LX + x
                own[z, x] = smooth_ref[n * 64 : n * 64 + 64, :]
        order = [(z, x) for z in range(LZ) for x in (2 * a, 2 * a + 1)]
        right = jnp.concatenate(
            [
                jnp.concatenate([jnp.where(even, across[k], zero), jnp.where(even, zero, across[k])], axis=1)
                for k in order
            ],
            axis=0,
        )
        sides = transposed_dot(jnp.concatenate([own[k] for k in order], axis=0), right)
        ends = [
            transposed_dot(
                jnp.concatenate([own[z, 2 * a], own[z, 2 * a + 1]], axis=0),
                jnp.concatenate([along[z, 2 * a], along[z, 2 * a + 1]], axis=0),
            )
            for z in range(LZ)
        ]
        rank = sum([(owners[b] == owners[a]).astype(jnp.int32) for b in range(a)], jnp.int32(0))
        slot = owners[a] * 2 + rank
        empty = jnp.zeros((128, 128), F32)
        out_ref[slot, :, 0:128] = part_ref[a, :, :128]
        second = combine(empty, sides[:, :128]).astype(BF16)
        out_ref[slot, :, 128:256] = jnp.where(low, part_ref[a, :, 128:], second)
        out_ref[slot, :, 256:384] = combine(sides[:, 128:], ends[0]).astype(BF16)
        out_ref[slot, :, 384:448] = combine(ends[1], empty).astype(BF16)[:, :64]


def vmem(count):
    return [pl.BlockSpec(memory_space=pltpu.VMEM)] * count


def paired(array):
    layers, across, length, width = array.shape
    lanes = array.transpose(0, 2, 1, 3).reshape(layers, length, across, width // 128, 128)
    return lanes.transpose(0, 1, 3, 2, 4)


def body(prolong, coupling, jacobi_scale, owner):
    tentative = paired(prolong).reshape(LZ * LX * 64, 128)
    blocks = paired(coupling).reshape(LZ * LX, 448, 128)
    scale = jacobi_scale.transpose(0, 2, 1, 3).reshape(LZ * LX * 2, 64)
    face = jax.ShapeDtypeStruct((LX * 2 * 32, 128), BF16)
    params = pltpu.CompilerParams(vmem_limit_bytes=40 * 2**20)
    smoothed, twice, zlo, zhi, ylo, yhi = pl.pallas_call(
        smooth_kernel,
        out_shape=(
            jax.ShapeDtypeStruct((LZ * LX * 64, 128), BF16),
            jax.ShapeDtypeStruct((LZ * LX, 128, 128), BF16),
            face,
            face,
            face,
            face,
        ),
        in_specs=vmem(3),
        out_specs=tuple(vmem(6)),
        compiler_params=params,
        name="smooth",
    )(tentative, blocks, scale)
    up = lambda a, axis: lax.ppermute(a, axis, [(i, i + 1) for i in range(lax.axis_size(axis) - 1)])
    down = lambda a, axis: lax.ppermute(a, axis, [(i + 1, i) for i in range(lax.axis_size(axis) - 1)])
    from_ylo, from_yhi = up(yhi, "col"), down(ylo, "col")
    from_zlo, from_zhi = up(zhi, "slab"), down(zlo, "slab")
    part = pl.pallas_call(
        local_kernel,
        out_shape=jax.ShapeDtypeStruct((LX // 2, 64, 256), BF16),
        in_specs=vmem(3),
        out_specs=vmem(1)[0],
        compiler_params=params,
        cost_estimate=pl.CostEstimate(flops=2 * 10**9, bytes_accessed=3 * 10**6, transcendentals=0),
        name="local_blocks",
    )(blocks, smoothed, twice)
    outgoing = pl.pallas_call(
        halo_kernel,
        out_shape=jax.ShapeDtypeStruct((8, 64, 448), BF16),
        in_specs=[pl.BlockSpec(memory_space=pltpu.SMEM)] + vmem(7),
        out_specs=vmem(1)[0],
        compiler_params=params,
        name="halo_blocks",
    )(owner, blocks, smoothed, part, from_zlo, from_zhi, from_ylo, from_yhi)
    incoming = lax.all_to_all(outgoing.reshape(4, 2, 64, 448), "col", split_axis=0, concat_axis=0, tiled=True)
    return incoming.reshape(8, 64, 448)


def solution(mesh):
    in_specs = (
        P("slab", "col", None, None),
        P("slab", "col", None, None),
        P("slab", "col", None, None),
        P(("slab", "col"), None),
    )
    out_specs = P(("slab", "col"), None, None)
    return jax.shard_map(body, mesh=mesh, in_specs=in_specs, out_specs=out_specs, check_vma=False)
```

```python
import jax
import jax.numpy as jnp
from jax import lax
from jax.experimental import pallas as pl
from jax.experimental.pallas import tpu as pltpu
from jax.sharding import PartitionSpec as P

FD = 64
LX = 6
LZ = 2
F32 = jnp.float32
BF16 = jnp.bfloat16


def low_lanes(rows):
    return lax.broadcasted_iota(jnp.int32, (rows, 128), 1) < 64


def even_rows(rows):
    return lax.broadcasted_iota(jnp.int32, (rows, 128), 0) % 2 == 0


def swap_halves(block):
    return jnp.concatenate([block[:, 64:], block[:, :64]], axis=1)


def unpairing():
    row = lax.broadcasted_iota(jnp.int32, (128, 128), 0)
    col = lax.broadcasted_iota(jnp.int32, (128, 128), 1)
    same_y = row // 64 == col % 2
    same_i = row % 64 == (col % 64) // 2 * 2 + col // 64
    return (same_y & same_i).astype(F32).astype(BF16)


def doubled(paired, matrix):
    swapped = swap_halves(paired)
    low = low_lanes(64)
    stacked = jnp.concatenate([jnp.where(low, paired, swapped), jnp.where(low, swapped, paired)], axis=0)
    return jnp.dot(matrix, stacked, preferred_element_type=F32).astype(BF16)


def diagonal(twice):
    low = low_lanes(64)
    zero = jnp.zeros_like(twice)
    return jnp.concatenate([jnp.where(low, twice, zero), jnp.where(low, zero, twice)], axis=0)


def diagonal_of_packed(packed):
    low = low_lanes(32)
    swapped = swap_halves(packed)
    zero = jnp.zeros_like(packed)
    return jnp.concatenate(
        [
            jnp.where(low, packed, zero),
            jnp.where(low, swapped, zero),
            jnp.where(low, zero, swapped),
            jnp.where(low, zero, packed),
        ],
        axis=0,
    )


def pick_y(both):
    return jnp.where(even_rows(64), both[:, :128], both[:, 128:])


def scales(s_ref, z):
    rows = LX * 64
    row = lax.broadcasted_iota(jnp.int32, (rows, 4 * LX), 0)
    col = lax.broadcasted_iota(jnp.int32, (rows, 4 * LX), 1)
    picks = (col == (row // 64 + z * LX) * 2 + row % 2).astype(F32).astype(BF16)
    spread = jnp.dot(picks, s_ref[...], preferred_element_type=F32)
    row = lax.broadcasted_iota(jnp.int32, (rows, 64), 0)
    col = lax.broadcasted_iota(jnp.int32, (rows, 64), 1)
    spread = jnp.where(row % 64 // 2 == col // 2, spread, 0.0).astype(BF16)
    row = lax.broadcasted_iota(jnp.int32, (64, 128), 0)
    col = lax.broadcasted_iota(jnp.int32, (64, 128), 1)
    halves = (row % 2 == col // 64).astype(F32).astype(BF16)
    return jnp.dot(spread, halves, preferred_element_type=F32)


def smooth_kernel(
    p_hbm, c_hbm, s_hbm, smooth_ref, twice_ref, zlo_ref, zhi_ref, ylo_ref, yhi_ref, p_ref, c_ref, s_ref, sems
):
    half = LX * 64
    scaling = pltpu.make_async_copy(s_hbm, s_ref, sems.at[4])
    scaling.start()
    layers = []
    for z in range(LZ):
        layers.append(
            (
                pltpu.make_async_copy(
                    p_hbm.at[z * half : z * half + half], p_ref.at[z * half : z * half + half], sems.at[2 * z]
                ),
                pltpu.make_async_copy(
                    c_hbm.at[z * LX : z * LX + LX, 0:64], c_ref.at[z * LX : z * LX + LX], sems.at[2 * z + 1]
                ),
            )
        )
        for copy in layers[z]:
            copy.start()
    matrix = unpairing()
    low = low_lanes(32)
    scaling.wait()
    scale = [scales(s_ref, z) for z in range(LZ)]
    for z in range(LZ):
        for copy in layers[z]:
            copy.wait()
        at = [z * half + x * 64 for x in range(LX)]
        tentative = [p_ref[r : r + 64, :] for r in at]
        twice = [doubled(block, matrix) for block in tentative]
        right = [jnp.concatenate([diagonal(t[:64]), diagonal(t[64:])], axis=1) for t in twice]
        both = [jnp.dot(c_ref[z * LX + x], right[x], preferred_element_type=F32) for x in range(LX)]
        smoothed = [
            (tentative[x].astype(F32) - scale[z][x * 64 : x * 64 + 64] * pick_y(both[x])).astype(BF16)
            for x in range(LX)
        ]
        twice = [doubled(block, matrix) for block in smoothed]
        for x in range(LX):
            smooth_ref[at[x] : at[x] + 64, :] = smoothed[x]
            twice_ref[z * LX + x] = twice[x]
            for y in range(2):
                packed = jnp.where(low, twice[x][y * 64 : y * 64 + 32], twice[x][y * 64 + 32 : y * 64 + 64])
                to = (x * 2 + y) * 32
                (zlo_ref, zhi_ref)[z][to : to + 32, :] = packed
                to = (z * LX + x) * 32
                (ylo_ref, yhi_ref)[y][to : to + 32, :] = packed


def combine(even, odd):
    low = low_lanes(64)
    return jnp.where(low, even[:64], odd[64:]) + swap_halves(jnp.where(low, odd[:64], even[64:]))


def transposed_dot(left, right):
    return lax.dot_general(left, right, (((0,), (0,)), ((), ())), preferred_element_type=F32)


def local_kernel(c_ref, smooth_ref, twice_ref, part_ref):
    def both_y(n, swapped=False):
        twice = twice_ref[n]
        first, second = diagonal(twice[:64]), diagonal(twice[64:])
        return jnp.concatenate([second, first] if swapped else [first, second], axis=1)

    even = even_rows(64)
    inner, outer = {}, {}
    for z in range(LZ):
        for x in range(LX):
            n = z * LX + x
            block = lambda d: c_ref[n, d * 64 : d * 64 + 64, :]
            across = jnp.where(even, block(4), block(3))
            left = jnp.concatenate([block(0), block(2 - x % 2), block(6 - z), across], axis=1)
            right = jnp.concatenate(
                [both_y(n), both_y(z * LX + (x ^ 1)), both_y((1 - z) * LX + x), both_y(n, True)], axis=0
            )
            inner[z, x] = pick_y(jnp.dot(left, right, preferred_element_type=F32)).astype(BF16)
            beside = x - 1 if x % 2 == 0 else x + 1
            if 0 <= beside < LX:
                outer[z, x] = pick_y(
                    jnp.dot(block(1 + x % 2), both_y(z * LX + beside), preferred_element_type=F32)
                ).astype(BF16)
    for a in range(LX // 2):
        own = {}
        for z in range(LZ):
            for x in (2 * a, 2 * a + 1):
                n = z * LX + x
                own[z, x] = smooth_ref[n * 64 : n * 64 + 64, :]
        order = [(z, x) for z in range(LZ) for x in (2 * a, 2 * a + 1)]
        total = transposed_dot(
            jnp.concatenate([own[k] for k in order], axis=0), jnp.concatenate([inner[k] for k in order], axis=0)
        )
        sides = []
        for x in (2 * a, 2 * a + 1):
            if (0, x) in outer:
                sides.append(
                    transposed_dot(
                        jnp.concatenate([own[0, x], own[1, x]], axis=0),
                        jnp.concatenate([outer[0, x], outer[1, x]], axis=0),
                    )
                )
            else:
                sides.append(jnp.zeros((128, 128), F32))
        part_ref[a, :, :128] = combine(total, sides[0]).astype(BF16)
        part_ref[a, :, 128:] = combine(sides[1], jnp.zeros((128, 128), F32)).astype(BF16)


def halo_kernel(owner_ref, c_ref, smooth_ref, part_ref, ylo_ref, yhi_ref, zlo_ref, zhi_ref, out_ref):
    even = even_rows(64)
    across, along = {}, {}
    for z in range(LZ):
        for x in range(LX):
            n = z * LX + x
            block = lambda d: c_ref[n, d * 64 : d * 64 + 64, :]
            right = jnp.concatenate(
                [diagonal_of_packed(ref[n * 32 : n * 32 + 32, :]) for ref in (ylo_ref, yhi_ref)], axis=1
            )
            left = jnp.where(even, block(3), block(4))
            across[z, x] = pick_y(jnp.dot(left, right, preferred_element_type=F32)).astype(BF16)
            ref = (zlo_ref, zhi_ref)[z]
            right = jnp.concatenate(
                [diagonal_of_packed(ref[(x * 2 + y) * 32 : (x * 2 + y) * 32 + 32, :]) for y in range(2)], axis=1
            )
            along[z, x] = pick_y(jnp.dot(block(5 + z), right, preferred_element_type=F32)).astype(BF16)
    out_ref[...] = jnp.zeros_like(out_ref)
    zero = jnp.zeros((64, 128), BF16)
    low = low_lanes(64)
    owners = [owner_ref[a, 0] for a in range(LX // 2)]
    for a in range(LX // 2):
        own = {}
        for z in range(LZ):
            for x in (2 * a, 2 * a + 1):
                n = z * LX + x
                own[z, x] = smooth_ref[n * 64 : n * 64 + 64, :]
        order = [(z, x) for z in range(LZ) for x in (2 * a, 2 * a + 1)]
        right = jnp.concatenate(
            [
                jnp.concatenate([jnp.where(even, across[k], zero), jnp.where(even, zero, across[k])], axis=1)
                for k in order
            ],
            axis=0,
        )
        sides = transposed_dot(jnp.concatenate([own[k] for k in order], axis=0), right)
        ends = [
            transposed_dot(
                jnp.concatenate([own[z, 2 * a], own[z, 2 * a + 1]], axis=0),
                jnp.concatenate([along[z, 2 * a], along[z, 2 * a + 1]], axis=0),
            )
            for z in range(LZ)
        ]
        rank = sum([(owners[b] == owners[a]).astype(jnp.int32) for b in range(a)], jnp.int32(0))
        slot = owners[a] * 2 + rank
        empty = jnp.zeros((128, 128), F32)
        out_ref[slot, 0:64, :] = part_ref[a, :, :128]
        second = combine(empty, sides[:, :128]).astype(BF16)
        out_ref[slot, 64:128, :] = jnp.where(low, part_ref[a, :, 128:], second)
        out_ref[slot, 128:192, :] = combine(sides[:, 128:], ends[0]).astype(BF16)
        last = combine(ends[1], ends[1]).astype(BF16)
        out_ref[slot, 192:224, :] = jnp.where(low[:32], last[:32], last[32:])


def unpack_kernel(in_ref, out_hbm, last_ref, sems):
    copies = [
        pltpu.make_async_copy(
            in_ref.at[:, p * 64 : p * 64 + 64, :], out_hbm.at[:, :, p * 128 : p * 128 + 128], sems.at[p]
        )
        for p in range(3)
    ]
    for copy in copies:
        copy.start()
    for slot in range(8):
        packed = in_ref[slot, 192:224, :]
        last_ref[slot, :32, :] = packed[:, :64]
        last_ref[slot, 32:, :] = packed[:, 64:]
    copies.append(pltpu.make_async_copy(last_ref, out_hbm.at[:, :, 384:448], sems.at[3]))
    copies[3].start()
    for copy in copies:
        copy.wait()


def vmem(count):
    return [pl.BlockSpec(memory_space=pltpu.VMEM)] * count


def paired(array):
    layers, across, length, width = array.shape
    lanes = array.transpose(0, 2, 1, 3).reshape(layers, length, across, width // 128, 128)
    return lanes.transpose(0, 1, 3, 2, 4)


def body(prolong, coupling, jacobi_scale, owner):
    tentative = paired(prolong).reshape(LZ * LX * 64, 128)
    blocks = paired(coupling).reshape(LZ * LX, 448, 128)
    scale = jacobi_scale.transpose(0, 2, 1, 3).reshape(LZ * LX * 2, 64)
    face = jax.ShapeDtypeStruct((LX * 2 * 32, 128), BF16)
    params = pltpu.CompilerParams(vmem_limit_bytes=40 * 2**20)
    smoothed, twice, zlo, zhi, ylo, yhi = pl.pallas_call(
        smooth_kernel,
        out_shape=(
            jax.ShapeDtypeStruct((LZ * LX * 64, 128), BF16),
            jax.ShapeDtypeStruct((LZ * LX, 128, 128), BF16),
            face,
            face,
            face,
            face,
        ),
        in_specs=[pl.BlockSpec(memory_space=pltpu.HBM)] * 3,
        out_specs=tuple(vmem(6)),
        scratch_shapes=[
            pltpu.VMEM((LZ * LX * 64, 128), BF16),
            pltpu.VMEM((LZ * LX, 64, 128), BF16),
            pltpu.VMEM((LZ * LX * 2, 64), BF16),
            pltpu.SemaphoreType.DMA((5,)),
        ],
        compiler_params=params,
        name="smooth",
    )(*(pltpu.with_memory_space_constraint(a, pltpu.HBM) for a in (tentative, blocks, scale)))
    up = lambda a, axis: lax.ppermute(a, axis, [(i, i + 1) for i in range(lax.axis_size(axis) - 1)])
    down = lambda a, axis: lax.ppermute(a, axis, [(i + 1, i) for i in range(lax.axis_size(axis) - 1)])
    from_zlo, from_zhi = up(zhi, "slab"), down(zlo, "slab")
    from_ylo, from_yhi = up(yhi, "col"), down(ylo, "col")
    part = pl.pallas_call(
        local_kernel,
        out_shape=jax.ShapeDtypeStruct((LX // 2, 64, 256), BF16),
        in_specs=vmem(3),
        out_specs=vmem(1)[0],
        compiler_params=params,
        cost_estimate=pl.CostEstimate(flops=2 * 10**9, bytes_accessed=3 * 10**6, transcendentals=0),
        name="local_blocks",
    )(blocks, smoothed, twice)
    outgoing = pl.pallas_call(
        halo_kernel,
        out_shape=jax.ShapeDtypeStruct((8, 224, 128), BF16),
        in_specs=[pl.BlockSpec(memory_space=pltpu.SMEM)] + vmem(7),
        out_specs=vmem(1)[0],
        compiler_params=params,
        name="halo_blocks",
    )(owner, blocks, smoothed, part, from_ylo, from_yhi, from_zlo, from_zhi)
    incoming = lax.all_to_all(outgoing.reshape(4, 448, 128), "col", split_axis=0, concat_axis=0, tiled=True)
    return pl.pallas_call(
        unpack_kernel,
        out_shape=jax.ShapeDtypeStruct((8, 64, 448), BF16),
        in_specs=vmem(1),
        out_specs=pl.BlockSpec(memory_space=pltpu.HBM),
        scratch_shapes=[pltpu.VMEM((8, 64, 64), BF16), pltpu.SemaphoreType.DMA((4,))],
        compiler_params=params,
        name="unpack",
    )(incoming.reshape(8, 224, 128))


def solution(mesh):
    in_specs = (
        P("slab", "col", None, None),
        P("slab", "col", None, None),
        P("slab", "col", None, None),
        P(("slab", "col"), None),
    )
    out_specs = P(("slab", "col"), None, None)
    return jax.shard_map(body, mesh=mesh, in_specs=in_specs, out_specs=out_specs, check_vma=False)
```

```python
import jax
import jax.numpy as jnp
from jax import lax
from jax.experimental import pallas as pl
from jax.experimental.pallas import tpu as pltpu
from jax.sharding import PartitionSpec as P

FD = 64
LX = 6
LZ = 2
F32 = jnp.float32
BF16 = jnp.bfloat16


def low_lanes(rows):
    return lax.broadcasted_iota(jnp.int32, (rows, 128), 1) < 64


def even_rows(rows):
    return lax.broadcasted_iota(jnp.int32, (rows, 128), 0) % 2 == 0


def swap_halves(block):
    return jnp.concatenate([block[:, 64:], block[:, :64]], axis=1)


def unpairing():
    row = lax.broadcasted_iota(jnp.int32, (128, 128), 0)
    col = lax.broadcasted_iota(jnp.int32, (128, 128), 1)
    same_y = row // 64 == col % 2
    same_i = row % 64 == (col % 64) // 2 * 2 + col // 64
    return (same_y & same_i).astype(F32).astype(BF16)


def doubled(blocks, matrix):
    low = low_lanes(64)
    stacked = []
    for paired in blocks:
        swapped = swap_halves(paired)
        stacked.append(jnp.concatenate([jnp.where(low, paired, swapped), jnp.where(low, swapped, paired)], axis=0))
    out = jnp.dot(matrix, jnp.concatenate(stacked, axis=1), preferred_element_type=F32).astype(BF16)
    return [out[:, n * 128 : n * 128 + 128] for n in range(len(blocks))]


def diagonal(twice):
    low = low_lanes(64)
    zero = jnp.zeros_like(twice)
    return jnp.concatenate([jnp.where(low, twice, zero), jnp.where(low, zero, twice)], axis=0)


def diagonal_of_packed(packed):
    low = low_lanes(32)
    swapped = swap_halves(packed)
    zero = jnp.zeros_like(packed)
    return jnp.concatenate(
        [
            jnp.where(low, packed, zero),
            jnp.where(low, swapped, zero),
            jnp.where(low, zero, swapped),
            jnp.where(low, zero, packed),
        ],
        axis=0,
    )


def pick_y(both):
    return jnp.where(even_rows(64), both[:, :128], both[:, 128:])


def scales(s_ref, z):
    rows = LX * 64
    row = lax.broadcasted_iota(jnp.int32, (rows, 4 * LX), 0)
    col = lax.broadcasted_iota(jnp.int32, (rows, 4 * LX), 1)
    picks = (col == (row // 64 + z * LX) * 2 + row % 2).astype(F32).astype(BF16)
    spread = jnp.dot(picks, s_ref[...], preferred_element_type=F32)
    row = lax.broadcasted_iota(jnp.int32, (rows, 64), 0)
    col = lax.broadcasted_iota(jnp.int32, (rows, 64), 1)
    spread = jnp.where(row % 64 // 2 == col // 2, spread, 0.0).astype(BF16)
    row = lax.broadcasted_iota(jnp.int32, (64, 128), 0)
    col = lax.broadcasted_iota(jnp.int32, (64, 128), 1)
    halves = (row % 2 == col // 64).astype(F32).astype(BF16)
    return jnp.dot(spread, halves, preferred_element_type=F32)


def smooth_kernel(
    p_hbm, c_hbm, s_hbm, o_hbm, smooth_ref, twice_ref, zlo_ref, zhi_ref, side_ref, p_ref, c_ref, d_ref, s_ref, o_ref, sems
):
    half = LX * 64
    scaling = pltpu.make_async_copy(s_hbm, s_ref, sems.at[6])
    naming = pltpu.make_async_copy(o_hbm, o_ref, sems.at[7])
    scaling.start()
    layers = []
    for z in range(LZ):
        rows, pairs = pl.ds(z * half, half), pl.ds(z * LX, LX)
        layers.append(
            (
                pltpu.make_async_copy(p_hbm.at[rows], p_ref.at[rows], sems.at[3 * z]),
                pltpu.make_async_copy(c_hbm.at[pairs, 0:64], c_ref.at[pairs], sems.at[3 * z + 1]),
                pltpu.make_async_copy(c_hbm.at[pairs, 192:256], d_ref.at[pairs], sems.at[3 * z + 2]),
            )
        )
        for copy in layers[z][:2]:
            copy.start()
    naming.start()
    for z in range(LZ):
        layers[z][2].start()
    matrix = unpairing()
    even = even_rows(64)
    low = low_lanes(32)
    zero = jnp.zeros((64, 128), BF16)
    scaling.wait()
    scale = [scales(s_ref, z) for z in range(LZ)]
    for z in range(LZ):
        for copy in layers[z][:2]:
            copy.wait()
        at = [z * half + x * 64 for x in range(LX)]
        tentative = [p_ref[r : r + 64, :] for r in at]
        twice = doubled(tentative, matrix)
        right = [jnp.concatenate([diagonal(t[:64]), diagonal(t[64:])], axis=1) for t in twice]
        both = [jnp.dot(c_ref[z * LX + x], right[x], preferred_element_type=F32) for x in range(LX)]
        smoothed = [
            (tentative[x].astype(F32) - scale[z][x * 64 : x * 64 + 64] * pick_y(both[x])).astype(BF16)
            for x in range(LX)
        ]
        twice = doubled(smoothed, matrix)
        layers[z][2].wait()
        left = [
            transposed_dot(jnp.where(even, d_ref[z * LX + x], zero), smoothed[x]) for x in range(LX)
        ]
        for x in range(0, LX, 2):
            to = (z * LX + x) * 32 + LZ * LX * 32
            side_ref[to : to + 64, :] = combine(left[x], left[x + 1]).astype(BF16)
        for x in range(LX):
            smooth_ref[at[x] : at[x] + 64, :] = smoothed[x]
            twice_ref[z * LX + x] = twice[x]
            for y in range(2):
                packed = jnp.where(low, twice[x][y * 64 : y * 64 + 32], twice[x][y * 64 + 32 : y * 64 + 64])
                to = (x * 2 + y) * 32
                (zlo_ref, zhi_ref)[z][to : to + 32, :] = packed
                if y == 0:
                    to = (z * LX + x) * 32
                    side_ref[to : to + 32, :] = packed
    naming.wait()
    owners = [jnp.broadcast_to(o_ref[:, a : a + 1], (16, 128)) for a in range(LX // 2)]
    for a in range(LX // 2):
        rank = sum([jnp.where(owners[b] == owners[a], 1, 0) for b in range(a)], jnp.zeros((16, 128), jnp.int32))
        slot = owners[a] * 2 + rank
        to = 2 * LZ * LX * 32 + a * 16
        side_ref[to : to + 16, :] = slot.astype(F32).astype(BF16)


def combine(even, odd):
    low = low_lanes(64)
    return jnp.where(low, even[:64], odd[64:]) + swap_halves(jnp.where(low, odd[:64], even[64:]))


def to_low(block):
    return block[:64] + swap_halves(block[64:])


def to_high(block):
    return swap_halves(block[:64]) + block[64:]


def transposed_dot(left, right):
    return lax.dot_general(left, right, (((0,), (0,)), ((), ())), preferred_element_type=F32)


def local_kernel(c_ref, smooth_ref, twice_ref, side_ref, part_ref, lent_ref):
    def both_y(n, swapped=False):
        twice = twice_ref[n]
        first, second = diagonal(twice[:64]), diagonal(twice[64:])
        return jnp.concatenate([second, first] if swapped else [first, second], axis=1)

    even = even_rows(64)
    zero = jnp.zeros((64, 128), BF16)
    inner, outer, across = {}, {}, {}
    for z in range(LZ):
        for x in range(LX):
            n = z * LX + x
            block = lambda d: c_ref[n, d * 64 : d * 64 + 64, :]
            mixed = jnp.where(even, block(4), block(3))
            left = jnp.concatenate([block(0), block(2 - x % 2), block(6 - z), mixed], axis=1)
            right = jnp.concatenate(
                [both_y(n), both_y(z * LX + (x ^ 1)), both_y((1 - z) * LX + x), both_y(n, True)], axis=0
            )
            inner[z, x] = pick_y(jnp.dot(left, right, preferred_element_type=F32)).astype(BF16)
            beside = x - 1 if x % 2 == 0 else x + 1
            if 0 <= beside < LX:
                outer[z, x] = pick_y(
                    jnp.dot(block(1 + x % 2), both_y(z * LX + beside), preferred_element_type=F32)
                ).astype(BF16)
            above = diagonal_of_packed(side_ref[n * 32 : n * 32 + 32, :])
            product = jnp.dot(block(4), above, preferred_element_type=F32).astype(BF16)
            across[z, x] = jnp.where(even, zero, product)
    for a in range(LX // 2):
        own = {}
        for z in range(LZ):
            for x in (2 * a, 2 * a + 1):
                n = z * LX + x
                own[z, x] = smooth_ref[n * 64 : n * 64 + 64, :]
        order = [(z, x) for z in range(LZ) for x in (2 * a, 2 * a + 1)]
        total = transposed_dot(
            jnp.concatenate([own[k] for k in order], axis=0),
            jnp.concatenate(
                [
                    jnp.concatenate([inner[k] for k in order], axis=0),
                    jnp.concatenate([across[k] for k in order], axis=0),
                ],
                axis=1,
            ),
        )
        sides = []
        for x in (2 * a, 2 * a + 1):
            if (0, x) in outer:
                sides.append(
                    transposed_dot(
                        jnp.concatenate([own[0, x], own[1, x]], axis=0),
                        jnp.concatenate([outer[0, x], outer[1, x]], axis=0),
                    )
                )
            else:
                sides.append(jnp.zeros((128, 128), F32))
        part_ref[a, 0:64, :] = combine(total[:, :128], sides[0]).astype(BF16)
        part_ref[a, 64:128, :] = to_low(total[:, 128:]).astype(BF16)
        part_ref[a, 128:192, :] = to_low(sides[1]).astype(BF16)
    low = low_lanes(32)
    lent = [jnp.zeros((32, 128), BF16)] * 8
    for a in range(LX // 2):
        begin = LZ * LX * 32
        left = jnp.concatenate(
            [side_ref[begin + (z * LX + 2 * a) * 32 : begin + (z * LX + 2 * a) * 32 + 64, :] for z in range(LZ)], axis=0
        )
        right = jnp.concatenate(
            [
                jnp.concatenate([twice_ref[z * LX + x, 64:, :] for z in range(LZ)], axis=0)
                for x in (2 * a, 2 * a + 1)
            ],
            axis=1,
        )
        product = transposed_dot(left, right)
        block = product[:64, :128] + product[64:, 128:]
        packed = jnp.where(low, block[:32], block[32:]).astype(BF16)
        slot = side_ref[2 * begin + a * 16 : 2 * begin + a * 16 + 16, :].astype(F32)
        slot = jnp.concatenate([slot, slot], axis=0)
        for place in range(8):
            lent[place] = jnp.where(slot == place, packed.astype(F32), lent[place].astype(F32)).astype(BF16)
    for place in range(8):
        lent_ref[place] = lent[place]


def halo_kernel(owner_ref, c_ref, smooth_ref, part_ref, lent_ref, zlo_ref, zhi_ref, out_ref):
    along = {}
    for z in range(LZ):
        for x in range(LX):
            n = z * LX + x
            ref = (zlo_ref, zhi_ref)[z]
            right = jnp.concatenate(
                [diagonal_of_packed(ref[(x * 2 + y) * 32 : (x * 2 + y) * 32 + 32, :]) for y in range(2)], axis=1
            )
            block = c_ref[n, (5 + z) * 64 : (6 + z) * 64, :]
            along[z, x] = pick_y(jnp.dot(block, right, preferred_element_type=F32)).astype(BF16)
    low = low_lanes(64)
    owners = [owner_ref[0, a] for a in range(LX // 2)]
    for place in range(8):
        out_ref[place, 0:192, :] = jnp.zeros((192, 128), BF16)
        out_ref[place, 192:224, :] = lent_ref[place]
    for a in range(LX // 2):
        ends = [
            to_high(
                transposed_dot(
                    jnp.concatenate(
                        [smooth_ref[(z * LX + x) * 64 : (z * LX + x) * 64 + 64, :] for x in (2 * a, 2 * a + 1)], axis=0
                    ),
                    jnp.concatenate([along[z, 2 * a], along[z, 2 * a + 1]], axis=0),
                )
            ).astype(BF16)
            for z in range(LZ)
        ]
        rank = sum([(owners[b] == owners[a]).astype(jnp.int32) for b in range(a)], jnp.int32(0))
        slot = owners[a] * 2 + rank
        out_ref[slot, 0:64, :] = part_ref[a, 0:64, :]
        out_ref[slot, 64:128, :] = jnp.where(low, part_ref[a, 64:128, :], ends[0])
        out_ref[slot, 128:192, :] = jnp.where(low, part_ref[a, 128:192, :], ends[1])


def unpack_kernel(in_ref, out_hbm, middle_ref, last_ref, sems):
    copies = [
        pltpu.make_async_copy(in_ref.at[:, 0:64, :], out_hbm.at[:, :, 0:128], sems.at[0]),
        pltpu.make_async_copy(in_ref.at[:, 64:128, :], out_hbm.at[:, :, 256:384], sems.at[1]),
    ]
    for copy in copies:
        copy.start()
    low = low_lanes(32)
    for slot in range(8):
        pair = in_ref[slot, 128:192, :]
        lent = in_ref[(slot + 6) % 8, 192:224, :]
        middle_ref[slot, :32, :] = jnp.where(low, pair[:32], swap_halves(lent))
        middle_ref[slot, 32:, :] = jnp.where(low, pair[32:], lent)
        last_ref[slot] = pair[:, 64:]
    copies.append(pltpu.make_async_copy(middle_ref, out_hbm.at[:, :, 128:256], sems.at[2]))
    copies.append(pltpu.make_async_copy(last_ref, out_hbm.at[:, :, 384:448], sems.at[3]))
    for copy in copies[2:]:
        copy.start()
    for copy in copies:
        copy.wait()


def vmem(count):
    return [pl.BlockSpec(memory_space=pltpu.VMEM)] * count


def paired(array):
    layers, across, length, width = array.shape
    lanes = array.transpose(0, 2, 1, 3).reshape(layers, length, across, width // 128, 128)
    return lanes.transpose(0, 1, 3, 2, 4)


def body(prolong, coupling, jacobi_scale, owner):
    tentative = paired(prolong).reshape(LZ * LX * 64, 128)
    blocks = paired(coupling).reshape(LZ * LX, 448, 128)
    scale = jacobi_scale.transpose(0, 2, 1, 3).reshape(LZ * LX * 2, 64)
    names = owner.T
    face = jax.ShapeDtypeStruct((LX * 2 * 32, 128), BF16)
    params = pltpu.CompilerParams(vmem_limit_bytes=40 * 2**20)
    arguments = (tentative, blocks, scale, names)
    smoothed, twice, zlo, zhi, side = pl.pallas_call(
        smooth_kernel,
        out_shape=(
            jax.ShapeDtypeStruct((LZ * LX * 64, 128), BF16),
            jax.ShapeDtypeStruct((LZ * LX, 128, 128), BF16),
            face,
            face,
            jax.ShapeDtypeStruct((2 * LZ * LX * 32 + 16 * (LX // 2), 128), BF16),
        ),
        in_specs=[pl.BlockSpec(memory_space=pltpu.HBM)] * 4,
        out_specs=tuple(vmem(5)),
        scratch_shapes=[
            pltpu.VMEM((LZ * LX * 64, 128), BF16),
            pltpu.VMEM((LZ * LX, 64, 128), BF16),
            pltpu.VMEM((LZ * LX, 64, 128), BF16),
            pltpu.VMEM((LZ * LX * 2, 64), BF16),
            pltpu.VMEM((1, LX // 2), jnp.int32),
            pltpu.SemaphoreType.DMA((8,)),
        ],
        compiler_params=params,
        name="smooth",
    )(*(pltpu.with_memory_space_constraint(a, pltpu.HBM) for a in arguments))
    up = lambda a, axis: lax.ppermute(a, axis, [(i, i + 1) for i in range(lax.axis_size(axis) - 1)])
    down = lambda a, axis: lax.ppermute(a, axis, [(i + 1, i) for i in range(lax.axis_size(axis) - 1)])
    from_zlo, from_zhi = up(zhi, "slab"), down(zlo, "slab")
    from_above = down(side, "col")
    part, lent = pl.pallas_call(
        local_kernel,
        out_shape=(
            jax.ShapeDtypeStruct((LX // 2, 192, 128), BF16),
            jax.ShapeDtypeStruct((8, 32, 128), BF16),
        ),
        in_specs=vmem(4),
        out_specs=tuple(vmem(2)),
        compiler_params=params,
        cost_estimate=pl.CostEstimate(flops=2 * 10**9, bytes_accessed=3 * 10**6, transcendentals=0),
        name="local_blocks",
    )(blocks, smoothed, twice, from_above)
    outgoing = pl.pallas_call(
        halo_kernel,
        out_shape=jax.ShapeDtypeStruct((8, 224, 128), BF16),
        in_specs=[pl.BlockSpec(memory_space=pltpu.SMEM)] + vmem(6),
        out_specs=vmem(1)[0],
        compiler_params=params,
        name="halo_blocks",
    )(names, blocks, smoothed, part, lent, from_zlo, from_zhi)
    incoming = lax.all_to_all(outgoing.reshape(4, 448, 128), "col", split_axis=0, concat_axis=0, tiled=True)
    return pl.pallas_call(
        unpack_kernel,
        out_shape=jax.ShapeDtypeStruct((8, 64, 448), BF16),
        in_specs=vmem(1),
        out_specs=pl.BlockSpec(memory_space=pltpu.HBM),
        scratch_shapes=[
            pltpu.VMEM((8, 64, 128), BF16),
            pltpu.VMEM((8, 64, 64), BF16),
            pltpu.SemaphoreType.DMA((4,)),
        ],
        compiler_params=params,
        name="unpack",
    )(incoming.reshape(8, 224, 128))


def solution(mesh):
    in_specs = (
        P("slab", "col", None, None),
        P("slab", "col", None, None),
        P("slab", "col", None, None),
        P(("slab", "col"), None),
    )
    out_specs = P(("slab", "col"), None, None)
    return jax.shard_map(body, mesh=mesh, in_specs=in_specs, out_specs=out_specs, check_vma=False)
```

```python
import jax
import jax.numpy as jnp
from jax import lax
from jax.experimental import pallas as pl
from jax.experimental.pallas import tpu as pltpu
from jax.sharding import PartitionSpec as P

FD = 64
LX = 6
LZ = 2
F32 = jnp.float32
BF16 = jnp.bfloat16


def low_lanes(rows):
    return lax.broadcasted_iota(jnp.int32, (rows, 128), 1) < 64


def even_rows(rows):
    return lax.broadcasted_iota(jnp.int32, (rows, 128), 0) % 2 == 0


def swap_halves(block):
    return jnp.concatenate([block[:, 64:], block[:, :64]], axis=1)


def unpairing():
    row = lax.broadcasted_iota(jnp.int32, (128, 128), 0)
    col = lax.broadcasted_iota(jnp.int32, (128, 128), 1)
    same_y = row // 64 == col % 2
    same_i = row % 64 == (col % 64) // 2 * 2 + col // 64
    return (same_y & same_i).astype(F32).astype(BF16)


def doubled(blocks, matrix):
    low = low_lanes(64)
    stacked = []
    for paired in blocks:
        swapped = swap_halves(paired)
        stacked.append(jnp.concatenate([jnp.where(low, paired, swapped), jnp.where(low, swapped, paired)], axis=0))
    out = jnp.dot(matrix, jnp.concatenate(stacked, axis=1), preferred_element_type=F32).astype(BF16)
    return [out[:, n * 128 : n * 128 + 128] for n in range(len(blocks))]


def diagonal(twice):
    low = low_lanes(64)
    zero = jnp.zeros_like(twice)
    return jnp.concatenate([jnp.where(low, twice, zero), jnp.where(low, zero, twice)], axis=0)


def diagonal_of_packed(packed):
    low = low_lanes(32)
    swapped = swap_halves(packed)
    zero = jnp.zeros_like(packed)
    return jnp.concatenate(
        [
            jnp.where(low, packed, zero),
            jnp.where(low, swapped, zero),
            jnp.where(low, zero, swapped),
            jnp.where(low, zero, packed),
        ],
        axis=0,
    )


def pick_y(both):
    return jnp.where(even_rows(64), both[:, :128], both[:, 128:])


def scales(s_ref, z):
    rows = LX * 64
    row = lax.broadcasted_iota(jnp.int32, (rows, 4 * LX), 0)
    col = lax.broadcasted_iota(jnp.int32, (rows, 4 * LX), 1)
    picks = (col == (row // 64 + z * LX) * 2 + row % 2).astype(F32).astype(BF16)
    spread = jnp.dot(picks, s_ref[...], preferred_element_type=F32)
    row = lax.broadcasted_iota(jnp.int32, (rows, 64), 0)
    col = lax.broadcasted_iota(jnp.int32, (rows, 64), 1)
    spread = jnp.where(row % 64 // 2 == col // 2, spread, 0.0).astype(BF16)
    row = lax.broadcasted_iota(jnp.int32, (64, 128), 0)
    col = lax.broadcasted_iota(jnp.int32, (64, 128), 1)
    halves = (row % 2 == col // 64).astype(F32).astype(BF16)
    return jnp.dot(spread, halves, preferred_element_type=F32)


def smooth_kernel(
    p_hbm, c_hbm, s_hbm, o_hbm, smooth_ref, twice_ref, zlo_ref, zhi_ref, side_ref, c_ref, p_ref, s_ref, o_ref, sems
):
    pairs = range(LZ * LX)
    scaling = pltpu.make_async_copy(s_hbm, s_ref, sems.at[0])
    reading = pltpu.make_async_copy(p_hbm, p_ref, sems.at[1])
    naming = pltpu.make_async_copy(o_hbm, o_ref, sems.at[2])
    first, third, second, last = [
        pltpu.make_async_copy(c_hbm.at[:, lo:hi], c_ref.at[:, lo:hi], sems.at[3 + n])
        for n, (lo, hi) in enumerate(((0, 64), (192, 256), (64, 192), (256, 448)))
    ]
    for copy in (scaling, reading, first, third, naming, second, last):
        copy.start()
    matrix = unpairing()
    even = even_rows(64)
    low = low_lanes(32)
    zero = jnp.zeros((64, 128), BF16)
    scaling.wait()
    scale = [scales(s_ref, z) for z in range(LZ)]
    reading.wait()
    tentative = [p_ref[n * 64 : n * 64 + 64, :] for n in pairs]
    twice = doubled(tentative, matrix)
    right = [jnp.concatenate([diagonal(t[:64]), diagonal(t[64:])], axis=1) for t in twice]
    first.wait()
    third.wait()
    both = [jnp.dot(c_ref[n, 0:64, :], right[n], preferred_element_type=F32) for n in pairs]
    smoothed = [
        (tentative[n].astype(F32) - scale[n // LX][n % LX * 64 : n % LX * 64 + 64] * pick_y(both[n])).astype(BF16)
        for n in pairs
    ]
    twice = doubled(smoothed, matrix)
    left = [transposed_dot(jnp.where(even, c_ref[n, 192:256, :], zero), smoothed[n]) for n in pairs]
    for n in range(0, LZ * LX, 2):
        to = (n + LZ * LX) * 32
        side_ref[to : to + 64, :] = combine(left[n], left[n + 1]).astype(BF16)
    for n in pairs:
        z, x = n // LX, n % LX
        smooth_ref[n * 64 : n * 64 + 64, :] = smoothed[n]
        twice_ref[n] = twice[n]
        for y in range(2):
            packed = jnp.where(low, twice[n][y * 64 : y * 64 + 32], twice[n][y * 64 + 32 : y * 64 + 64])
            to = (x * 2 + y) * 32
            (zlo_ref, zhi_ref)[z][to : to + 32, :] = packed
            if y == 0:
                side_ref[n * 32 : n * 32 + 32, :] = packed
    naming.wait()
    owners = [jnp.broadcast_to(o_ref[:, a : a + 1], (16, 128)) for a in range(LX // 2)]
    for a in range(LX // 2):
        rank = sum([jnp.where(owners[b] == owners[a], 1, 0) for b in range(a)], jnp.zeros((16, 128), jnp.int32))
        slot = owners[a] * 2 + rank
        to = 2 * LZ * LX * 32 + a * 16
        side_ref[to : to + 16, :] = slot.astype(F32).astype(BF16)
    second.wait()
    last.wait()


def combine(even, odd):
    low = low_lanes(64)
    return jnp.where(low, even[:64], odd[64:]) + swap_halves(jnp.where(low, odd[:64], even[64:]))


def to_low(block):
    return block[:64] + swap_halves(block[64:])


def to_high(block):
    return swap_halves(block[:64]) + block[64:]


def transposed_dot(left, right):
    return lax.dot_general(left, right, (((0,), (0,)), ((), ())), preferred_element_type=F32)


def local_kernel(c_ref, smooth_ref, twice_ref, side_ref, part_ref, lent_ref, turned_ref):
    def both_y(n, swapped=False):
        twice = twice_ref[n]
        first, second = diagonal(twice[:64]), diagonal(twice[64:])
        return jnp.concatenate([second, first] if swapped else [first, second], axis=1)

    even = even_rows(64)
    zero = jnp.zeros((64, 128), BF16)
    inner, outer, across = {}, {}, {}
    for z in range(LZ):
        for x in range(LX):
            n = z * LX + x
            block = lambda d: c_ref[n, d * 64 : d * 64 + 64, :]
            mixed = jnp.where(even, block(4), block(3))
            left = jnp.concatenate([block(0), block(2 - x % 2), block(6 - z), mixed], axis=1)
            right = jnp.concatenate(
                [both_y(n), both_y(z * LX + (x ^ 1)), both_y((1 - z) * LX + x), both_y(n, True)], axis=0
            )
            inner[z, x] = pick_y(jnp.dot(left, right, preferred_element_type=F32)).astype(BF16)
            beside = x - 1 if x % 2 == 0 else x + 1
            if 0 <= beside < LX:
                outer[z, x] = pick_y(
                    jnp.dot(block(1 + x % 2), both_y(z * LX + beside), preferred_element_type=F32)
                ).astype(BF16)
            above = diagonal_of_packed(side_ref[n * 32 : n * 32 + 32, :])
            product = jnp.dot(block(4), above, preferred_element_type=F32).astype(BF16)
            across[z, x] = jnp.where(even, zero, product)
    nothing = jnp.zeros((64, 128), BF16)
    for a in range(LX // 2):
        turned = []
        for z in range(LZ):
            begin = (z * LX + 2 * a) * 64
            turned.append(smooth_ref[begin : begin + 128, :].T)
            turned_ref[a, z] = turned[z]
        right = []
        for z in range(LZ):
            for x in (2 * a, 2 * a + 1):
                beside = outer.get((z, x), nothing)
                ends = [beside, nothing] if x % 2 == 0 else [nothing, beside]
                right.append(jnp.concatenate([inner[z, x], across[z, x]] + ends, axis=1))
        total = jnp.dot(
            jnp.concatenate(turned, axis=1), jnp.concatenate(right, axis=0), preferred_element_type=F32
        )
        part_ref[a, 0:64, :] = combine(total[:, :128], total[:, 256:384]).astype(BF16)
        part_ref[a, 64:128, :] = to_low(total[:, 128:256]).astype(BF16)
        part_ref[a, 128:192, :] = to_low(total[:, 384:]).astype(BF16)
    low = low_lanes(32)
    lent = [jnp.zeros((32, 128), BF16)] * 8
    for a in range(LX // 2):
        begin = LZ * LX * 32
        left = jnp.concatenate(
            [side_ref[begin + (z * LX + 2 * a) * 32 : begin + (z * LX + 2 * a) * 32 + 64, :] for z in range(LZ)], axis=0
        )
        right = jnp.concatenate(
            [
                jnp.concatenate([twice_ref[z * LX + x, 64:, :] for z in range(LZ)], axis=0)
                for x in (2 * a, 2 * a + 1)
            ],
            axis=1,
        )
        product = transposed_dot(left, right)
        block = product[:64, :128] + product[64:, 128:]
        packed = jnp.where(low, block[:32], block[32:]).astype(BF16)
        slot = side_ref[2 * begin + a * 16 : 2 * begin + a * 16 + 16, :].astype(F32)
        slot = jnp.concatenate([slot, slot], axis=0)
        for place in range(8):
            lent[place] = jnp.where(slot == place, packed.astype(F32), lent[place].astype(F32)).astype(BF16)
    for place in range(8):
        lent_ref[place] = lent[place]


def halo_kernel(owner_ref, c_ref, turned_ref, part_ref, lent_ref, zlo_ref, zhi_ref, out_ref):
    along = {}
    for z in range(LZ):
        for x in range(LX):
            n = z * LX + x
            ref = (zlo_ref, zhi_ref)[z]
            right = jnp.concatenate(
                [diagonal_of_packed(ref[(x * 2 + y) * 32 : (x * 2 + y) * 32 + 32, :]) for y in range(2)], axis=1
            )
            block = c_ref[n, (5 + z) * 64 : (6 + z) * 64, :]
            along[z, x] = pick_y(jnp.dot(block, right, preferred_element_type=F32)).astype(BF16)
    low = low_lanes(64)
    owners = [owner_ref[0, a] for a in range(LX // 2)]
    for place in range(8):
        out_ref[place, 0:192, :] = jnp.zeros((192, 128), BF16)
        out_ref[place, 192:224, :] = lent_ref[place]
    for a in range(LX // 2):
        ends = [
            to_high(
                jnp.dot(
                    turned_ref[a, z],
                    jnp.concatenate([along[z, 2 * a], along[z, 2 * a + 1]], axis=0),
                    preferred_element_type=F32,
                )
            ).astype(BF16)
            for z in range(LZ)
        ]
        rank = sum([(owners[b] == owners[a]).astype(jnp.int32) for b in range(a)], jnp.int32(0))
        slot = owners[a] * 2 + rank
        out_ref[slot, 0:64, :] = part_ref[a, 0:64, :]
        out_ref[slot, 64:128, :] = jnp.where(low, part_ref[a, 64:128, :], ends[0])
        out_ref[slot, 128:192, :] = jnp.where(low, part_ref[a, 128:192, :], ends[1])


def unpack_kernel(in_ref, out_hbm, middle_ref, last_ref, sems):
    copies = [
        pltpu.make_async_copy(in_ref.at[:, 0:64, :], out_hbm.at[:, :, 0:128], sems.at[0]),
        pltpu.make_async_copy(in_ref.at[:, 64:128, :], out_hbm.at[:, :, 256:384], sems.at[1]),
    ]
    for copy in copies:
        copy.start()
    low = low_lanes(32)
    for slot in range(8):
        pair = in_ref[slot, 128:192, :]
        lent = in_ref[(slot + 6) % 8, 192:224, :]
        middle_ref[slot, :32, :] = jnp.where(low, pair[:32], swap_halves(lent))
        middle_ref[slot, 32:, :] = jnp.where(low, pair[32:], lent)
        last_ref[slot] = pair[:, 64:]
    copies.append(pltpu.make_async_copy(middle_ref, out_hbm.at[:, :, 128:256], sems.at[2]))
    copies.append(pltpu.make_async_copy(last_ref, out_hbm.at[:, :, 384:448], sems.at[3]))
    for copy in copies[2:]:
        copy.start()
    for copy in copies:
        copy.wait()


def vmem(count):
    return [pl.BlockSpec(memory_space=pltpu.VMEM)] * count


def paired(array):
    layers, across, length, width = array.shape
    lanes = array.transpose(0, 2, 1, 3).reshape(layers, length, across, width // 128, 128)
    return lanes.transpose(0, 1, 3, 2, 4)


def body(prolong, coupling, jacobi_scale, owner):
    tentative = paired(prolong).reshape(LZ * LX * 64, 128)
    blocks = paired(coupling).reshape(LZ * LX, 448, 128)
    scale = jacobi_scale.transpose(0, 2, 1, 3).reshape(LZ * LX * 2, 64)
    names = owner.T
    face = jax.ShapeDtypeStruct((LX * 2 * 32, 128), BF16)
    params = pltpu.CompilerParams(vmem_limit_bytes=40 * 2**20)
    arguments = (tentative, blocks, scale, names)
    smoothed, twice, zlo, zhi, side, held = pl.pallas_call(
        smooth_kernel,
        out_shape=(
            jax.ShapeDtypeStruct((LZ * LX * 64, 128), BF16),
            jax.ShapeDtypeStruct((LZ * LX, 128, 128), BF16),
            face,
            face,
            jax.ShapeDtypeStruct((2 * LZ * LX * 32 + 16 * (LX // 2), 128), BF16),
            jax.ShapeDtypeStruct((LZ * LX, 448, 128), BF16),
        ),
        in_specs=[pl.BlockSpec(memory_space=pltpu.HBM)] * 4,
        out_specs=tuple(vmem(6)),
        scratch_shapes=[
            pltpu.VMEM((LZ * LX * 64, 128), BF16),
            pltpu.VMEM((LZ * LX * 2, 64), BF16),
            pltpu.VMEM((1, LX // 2), jnp.int32),
            pltpu.SemaphoreType.DMA((7,)),
        ],
        compiler_params=params,
        name="smooth",
    )(*(pltpu.with_memory_space_constraint(a, pltpu.HBM) for a in arguments))
    up = lambda a, axis: lax.ppermute(a, axis, [(i, i + 1) for i in range(lax.axis_size(axis) - 1)])
    down = lambda a, axis: lax.ppermute(a, axis, [(i + 1, i) for i in range(lax.axis_size(axis) - 1)])
    from_zlo, from_zhi = up(zhi, "slab"), down(zlo, "slab")
    from_above = down(side, "col")
    part, lent, turned = pl.pallas_call(
        local_kernel,
        out_shape=(
            jax.ShapeDtypeStruct((LX // 2, 192, 128), BF16),
            jax.ShapeDtypeStruct((8, 32, 128), BF16),
            jax.ShapeDtypeStruct((LX // 2, LZ, 128, 128), BF16),
        ),
        in_specs=vmem(4),
        out_specs=tuple(vmem(3)),
        compiler_params=params,
        cost_estimate=pl.CostEstimate(flops=2 * 10**9, bytes_accessed=3 * 10**6, transcendentals=0),
        name="local_blocks",
    )(held, smoothed, twice, from_above)
    outgoing = pl.pallas_call(
        halo_kernel,
        out_shape=jax.ShapeDtypeStruct((8, 224, 128), BF16),
        in_specs=[pl.BlockSpec(memory_space=pltpu.SMEM)] + vmem(6),
        out_specs=vmem(1)[0],
        compiler_params=params,
        name="halo_blocks",
    )(names, held, turned, part, lent, from_zlo, from_zhi)
    incoming = lax.all_to_all(outgoing.reshape(4, 448, 128), "col", split_axis=0, concat_axis=0, tiled=True)
    return pl.pallas_call(
        unpack_kernel,
        out_shape=jax.ShapeDtypeStruct((8, 64, 448), BF16),
        in_specs=vmem(1),
        out_specs=pl.BlockSpec(memory_space=pltpu.HBM),
        scratch_shapes=[
            pltpu.VMEM((8, 64, 128), BF16),
            pltpu.VMEM((8, 64, 64), BF16),
            pltpu.SemaphoreType.DMA((4,)),
        ],
        compiler_params=params,
        name="unpack",
    )(incoming.reshape(8, 224, 128))


def solution(mesh):
    in_specs = (
        P("slab", "col", None, None),
        P("slab", "col", None, None),
        P("slab", "col", None, None),
        P(("slab", "col"), None),
    )
    out_specs = P(("slab", "col"), None, None)
    return jax.shard_map(body, mesh=mesh, in_specs=in_specs, out_specs=out_specs, check_vma=False)
```

```python
import jax
import jax.numpy as jnp
from jax import lax
from jax.experimental import pallas as pl
from jax.experimental.pallas import tpu as pltpu
from jax.sharding import PartitionSpec as P

FD = 64
LX = 6
LZ = 2
F32 = jnp.float32
BF16 = jnp.bfloat16


def low_lanes(rows):
    return lax.broadcasted_iota(jnp.int32, (rows, 128), 1) < 64


def even_rows(rows):
    return lax.broadcasted_iota(jnp.int32, (rows, 128), 0) % 2 == 0


def swap_halves(block):
    return jnp.concatenate([block[:, 64:], block[:, :64]], axis=1)


def unpairing():
    row = lax.broadcasted_iota(jnp.int32, (128, 128), 0)
    col = lax.broadcasted_iota(jnp.int32, (128, 128), 1)
    same_y = row // 64 == col % 2
    same_i = row % 64 == (col % 64) // 2 * 2 + col // 64
    return (same_y & same_i).astype(F32).astype(BF16)


def doubled(blocks, matrix):
    low = low_lanes(64)
    stacked = []
    for paired in blocks:
        swapped = swap_halves(paired)
        stacked.append(jnp.concatenate([jnp.where(low, paired, swapped), jnp.where(low, swapped, paired)], axis=0))
    out = jnp.dot(matrix, jnp.concatenate(stacked, axis=1), preferred_element_type=F32).astype(BF16)
    return [out[:, n * 128 : n * 128 + 128] for n in range(len(blocks))]


def diagonal(twice):
    low = low_lanes(64)
    zero = jnp.zeros_like(twice)
    return jnp.concatenate([jnp.where(low, twice, zero), jnp.where(low, zero, twice)], axis=0)


def diagonal_of_packed(packed):
    low = low_lanes(32)
    swapped = swap_halves(packed)
    zero = jnp.zeros_like(packed)
    return jnp.concatenate(
        [
            jnp.where(low, packed, zero),
            jnp.where(low, swapped, zero),
            jnp.where(low, zero, swapped),
            jnp.where(low, zero, packed),
        ],
        axis=0,
    )


def pick_y(both):
    return jnp.where(even_rows(64), both[:, :128], both[:, 128:])


def scales(s_ref, z):
    rows = LX * 64
    row = lax.broadcasted_iota(jnp.int32, (rows, 4 * LX), 0)
    col = lax.broadcasted_iota(jnp.int32, (rows, 4 * LX), 1)
    picks = (col == (row // 64 + z * LX) * 2 + row % 2).astype(F32).astype(BF16)
    spread = jnp.dot(picks, s_ref[...], preferred_element_type=F32)
    row = lax.broadcasted_iota(jnp.int32, (rows, 64), 0)
    col = lax.broadcasted_iota(jnp.int32, (rows, 64), 1)
    spread = jnp.where(row % 64 // 2 == col // 2, spread, 0.0).astype(BF16)
    row = lax.broadcasted_iota(jnp.int32, (64, 128), 0)
    col = lax.broadcasted_iota(jnp.int32, (64, 128), 1)
    halves = (row % 2 == col // 64).astype(F32).astype(BF16)
    return jnp.dot(spread, halves, preferred_element_type=F32)


def smooth_kernel(
    p_hbm, c_hbm, s_hbm, o_hbm, smooth_ref, twice_ref, zlo_ref, zhi_ref, side_ref, c_ref, p_ref, s_ref, o_ref, sems
):
    pairs = range(LZ * LX)
    scaling = pltpu.make_async_copy(s_hbm, s_ref, sems.at[0])
    reading = pltpu.make_async_copy(p_hbm, p_ref, sems.at[1])
    naming = pltpu.make_async_copy(o_hbm, o_ref, sems.at[2])
    first, third, second, last = [
        pltpu.make_async_copy(c_hbm.at[:, lo:hi], c_ref.at[:, lo:hi], sems.at[3 + n])
        for n, (lo, hi) in enumerate(((0, 64), (192, 256), (64, 192), (256, 448)))
    ]
    for copy in (scaling, reading, first, third, naming, second, last):
        copy.start()
    matrix = unpairing()
    even = even_rows(64)
    low = low_lanes(32)
    zero = jnp.zeros((64, 128), BF16)
    scaling.wait()
    scale = [scales(s_ref, z) for z in range(LZ)]
    reading.wait()
    tentative = [p_ref[n * 64 : n * 64 + 64, :] for n in pairs]
    twice = doubled(tentative, matrix)
    right = [jnp.concatenate([diagonal(t[:64]), diagonal(t[64:])], axis=1) for t in twice]
    first.wait()
    third.wait()
    both = [jnp.dot(c_ref[n, 0:64, :], right[n], preferred_element_type=F32) for n in pairs]
    smoothed = [
        (tentative[n].astype(F32) - scale[n // LX][n % LX * 64 : n % LX * 64 + 64] * pick_y(both[n])).astype(BF16)
        for n in pairs
    ]
    twice = doubled(smoothed, matrix)
    left = [transposed_dot(jnp.where(even, c_ref[n, 192:256, :], zero), smoothed[n]) for n in pairs]
    for n in range(0, LZ * LX, 2):
        to = (n + LZ * LX) * 32
        side_ref[to : to + 64, :] = combine(left[n], left[n + 1]).astype(BF16)
    for n in pairs:
        z, x = n // LX, n % LX
        smooth_ref[n * 64 : n * 64 + 64, :] = smoothed[n]
        twice_ref[n] = twice[n]
        for y in range(2):
            packed = jnp.where(low, twice[n][y * 64 : y * 64 + 32], twice[n][y * 64 + 32 : y * 64 + 64])
            to = (x * 2 + y) * 32
            (zlo_ref, zhi_ref)[z][to : to + 32, :] = packed
            if y == 0:
                side_ref[n * 32 : n * 32 + 32, :] = packed
    naming.wait()
    owners = [jnp.broadcast_to(o_ref[:, a : a + 1], (16, 128)) for a in range(LX // 2)]
    for a in range(LX // 2):
        rank = sum([jnp.where(owners[b] == owners[a], 1, 0) for b in range(a)], jnp.zeros((16, 128), jnp.int32))
        slot = owners[a] * 2 + rank
        to = 2 * LZ * LX * 32 + a * 16
        side_ref[to : to + 16, :] = slot.astype(F32).astype(BF16)
    second.wait()
    last.wait()


def combine(even, odd):
    low = low_lanes(64)
    return jnp.where(low, even[:64], odd[64:]) + swap_halves(jnp.where(low, odd[:64], even[64:]))


def to_low(block):
    return block[:64] + swap_halves(block[64:])


def to_high(block):
    return swap_halves(block[:64]) + block[64:]


def transposed_dot(left, right):
    return lax.dot_general(left, right, (((0,), (0,)), ((), ())), preferred_element_type=F32)


def along_z(z, halo_ref, c_ref, turned, a):
    products = []
    for x in (2 * a, 2 * a + 1):
        right = jnp.concatenate(
            [diagonal_of_packed(halo_ref[(x * 2 + y) * 32 : (x * 2 + y) * 32 + 32, :]) for y in range(2)], axis=1
        )
        block = c_ref[z * LX + x, (5 + z) * 64 : (6 + z) * 64, :]
        products.append(pick_y(jnp.dot(block, right, preferred_element_type=F32)).astype(BF16))
    return to_high(jnp.dot(turned, jnp.concatenate(products, axis=0), preferred_element_type=F32))


def local_kernel(c_ref, smooth_ref, twice_ref, side_ref, zlo_ref, part_ref, lent_ref, turned_ref):
    def both_y(n, swapped=False):
        twice = twice_ref[n]
        first, second = diagonal(twice[:64]), diagonal(twice[64:])
        return jnp.concatenate([second, first] if swapped else [first, second], axis=1)

    even = even_rows(64)
    zero = jnp.zeros((64, 128), BF16)
    inner, outer, across = {}, {}, {}
    for z in range(LZ):
        for x in range(LX):
            n = z * LX + x
            block = lambda d: c_ref[n, d * 64 : d * 64 + 64, :]
            mixed = jnp.where(even, block(4), block(3))
            left = jnp.concatenate([block(0), block(2 - x % 2), block(6 - z), mixed], axis=1)
            right = jnp.concatenate(
                [both_y(n), both_y(z * LX + (x ^ 1)), both_y((1 - z) * LX + x), both_y(n, True)], axis=0
            )
            inner[z, x] = pick_y(jnp.dot(left, right, preferred_element_type=F32)).astype(BF16)
            beside = x - 1 if x % 2 == 0 else x + 1
            if 0 <= beside < LX:
                outer[z, x] = pick_y(
                    jnp.dot(block(1 + x % 2), both_y(z * LX + beside), preferred_element_type=F32)
                ).astype(BF16)
            above = diagonal_of_packed(side_ref[n * 32 : n * 32 + 32, :])
            product = jnp.dot(block(4), above, preferred_element_type=F32).astype(BF16)
            across[z, x] = jnp.where(even, zero, product)
    nothing = jnp.zeros((64, 128), BF16)
    for a in range(LX // 2):
        turned = []
        for z in range(LZ):
            begin = (z * LX + 2 * a) * 64
            turned.append(smooth_ref[begin : begin + 128, :].T)
            turned_ref[a, z] = turned[z]
        right = []
        for z in range(LZ):
            for x in (2 * a, 2 * a + 1):
                beside = outer.get((z, x), nothing)
                ends = [beside, nothing] if x % 2 == 0 else [nothing, beside]
                right.append(jnp.concatenate([inner[z, x], across[z, x]] + ends, axis=1))
        total = jnp.dot(
            jnp.concatenate(turned, axis=1), jnp.concatenate(right, axis=0), preferred_element_type=F32
        )
        part_ref[a, 0:64, :] = combine(total[:, :128], total[:, 256:384]).astype(BF16)
        beyond = along_z(0, zlo_ref, c_ref, turned[0], a)
        part_ref[a, 64:128, :] = jnp.where(low_lanes(64), to_low(total[:, 128:256]), beyond).astype(BF16)
        part_ref[a, 128:192, :] = to_low(total[:, 384:]).astype(BF16)
    low = low_lanes(32)
    lent = [jnp.zeros((32, 128), BF16)] * 8
    for a in range(LX // 2):
        begin = LZ * LX * 32
        left = jnp.concatenate(
            [side_ref[begin + (z * LX + 2 * a) * 32 : begin + (z * LX + 2 * a) * 32 + 64, :] for z in range(LZ)], axis=0
        )
        right = jnp.concatenate(
            [
                jnp.concatenate([twice_ref[z * LX + x, 64:, :] for z in range(LZ)], axis=0)
                for x in (2 * a, 2 * a + 1)
            ],
            axis=1,
        )
        product = transposed_dot(left, right)
        block = product[:64, :128] + product[64:, 128:]
        packed = jnp.where(low, block[:32], block[32:]).astype(BF16)
        slot = side_ref[2 * begin + a * 16 : 2 * begin + a * 16 + 16, :].astype(F32)
        slot = jnp.concatenate([slot, slot], axis=0)
        for place in range(8):
            lent[place] = jnp.where(slot == place, packed.astype(F32), lent[place].astype(F32)).astype(BF16)
    for place in range(8):
        lent_ref[place] = lent[place]


def halo_kernel(c_ref, turned_ref, part_ref, lent_ref, own_ref, zhi_ref, out_ref):
    low = low_lanes(64)
    begin = 2 * LZ * LX * 32
    slots = [own_ref[begin + a * 16 : begin + a * 16 + 16, :].astype(F32) for a in range(LX // 2)]
    here = [[jnp.where(slot == place, 1.0, 0.0).astype(BF16) for slot in slots] for place in range(8)]

    def placed(blocks, place):
        count = blocks[0].shape[0] // 16
        masks = [jnp.concatenate([mask] * count, axis=0) for mask in here[place]]
        return sum([masks[a] * blocks[a] for a in range(1, LX // 2)], masks[0] * blocks[0])

    last = [along_z(1, zhi_ref, c_ref, turned_ref[a, 1], a).astype(BF16) for a in range(LX // 2)]
    ready = [part_ref[a, 0:128, :] for a in range(LX // 2)]
    for place in range(8):
        out_ref[place, 0:128, :] = placed(ready, place)
        out_ref[place, 192:224, :] = lent_ref[place]
    pair = [jnp.where(low, part_ref[a, 128:192, :], last[a]) for a in range(LX // 2)]
    for place in range(8):
        out_ref[place, 128:192, :] = placed(pair, place)


def unpack_kernel(in_ref, out_hbm, middle_ref, last_ref, sems):
    copies = [
        pltpu.make_async_copy(in_ref.at[:, 0:64, :], out_hbm.at[:, :, 0:128], sems.at[0]),
        pltpu.make_async_copy(in_ref.at[:, 64:128, :], out_hbm.at[:, :, 256:384], sems.at[1]),
    ]
    for copy in copies:
        copy.start()
    low = low_lanes(32)
    for slot in range(8):
        pair = in_ref[slot, 128:192, :]
        lent = in_ref[(slot + 6) % 8, 192:224, :]
        middle_ref[slot, :32, :] = jnp.where(low, pair[:32], swap_halves(lent))
        middle_ref[slot, 32:, :] = jnp.where(low, pair[32:], lent)
        last_ref[slot] = pair[:, 64:]
    copies.append(pltpu.make_async_copy(middle_ref, out_hbm.at[:, :, 128:256], sems.at[2]))
    copies.append(pltpu.make_async_copy(last_ref, out_hbm.at[:, :, 384:448], sems.at[3]))
    for copy in copies[2:]:
        copy.start()
    for copy in copies:
        copy.wait()


def vmem(count):
    return [pl.BlockSpec(memory_space=pltpu.VMEM)] * count


def paired(array):
    layers, across, length, width = array.shape
    lanes = array.transpose(0, 2, 1, 3).reshape(layers, length, across, width // 128, 128)
    return lanes.transpose(0, 1, 3, 2, 4)


def body(prolong, coupling, jacobi_scale, owner):
    tentative = paired(prolong).reshape(LZ * LX * 64, 128)
    blocks = paired(coupling).reshape(LZ * LX, 448, 128)
    scale = jacobi_scale.transpose(0, 2, 1, 3).reshape(LZ * LX * 2, 64)
    names = owner.T
    face = jax.ShapeDtypeStruct((LX * 2 * 32, 128), BF16)
    params = pltpu.CompilerParams(vmem_limit_bytes=40 * 2**20)
    arguments = (tentative, blocks, scale, names)
    smoothed, twice, zlo, zhi, side, held = pl.pallas_call(
        smooth_kernel,
        out_shape=(
            jax.ShapeDtypeStruct((LZ * LX * 64, 128), BF16),
            jax.ShapeDtypeStruct((LZ * LX, 128, 128), BF16),
            face,
            face,
            jax.ShapeDtypeStruct((2 * LZ * LX * 32 + 16 * (LX // 2), 128), BF16),
            jax.ShapeDtypeStruct((LZ * LX, 448, 128), BF16),
        ),
        in_specs=[pl.BlockSpec(memory_space=pltpu.HBM)] * 4,
        out_specs=tuple(vmem(6)),
        scratch_shapes=[
            pltpu.VMEM((LZ * LX * 64, 128), BF16),
            pltpu.VMEM((LZ * LX * 2, 64), BF16),
            pltpu.VMEM((1, LX // 2), jnp.int32),
            pltpu.SemaphoreType.DMA((7,)),
        ],
        compiler_params=params,
        name="smooth",
    )(*(pltpu.with_memory_space_constraint(a, pltpu.HBM) for a in arguments))
    up = lambda a, axis: lax.ppermute(a, axis, [(i, i + 1) for i in range(lax.axis_size(axis) - 1)])
    down = lambda a, axis: lax.ppermute(a, axis, [(i + 1, i) for i in range(lax.axis_size(axis) - 1)])
    from_zlo, from_zhi = up(zhi, "slab"), down(zlo, "slab")
    from_above = down(side, "col")
    part, lent, turned = pl.pallas_call(
        local_kernel,
        out_shape=(
            jax.ShapeDtypeStruct((LX // 2, 192, 128), BF16),
            jax.ShapeDtypeStruct((8, 32, 128), BF16),
            jax.ShapeDtypeStruct((LX // 2, LZ, 128, 128), BF16),
        ),
        in_specs=vmem(5),
        out_specs=tuple(vmem(3)),
        compiler_params=params,
        cost_estimate=pl.CostEstimate(flops=2 * 10**9, bytes_accessed=3 * 10**6, transcendentals=0),
        name="local_blocks",
    )(held, smoothed, twice, from_above, from_zlo)
    outgoing = pl.pallas_call(
        halo_kernel,
        out_shape=jax.ShapeDtypeStruct((8, 224, 128), BF16),
        in_specs=vmem(6),
        out_specs=vmem(1)[0],
        compiler_params=params,
        name="halo_blocks",
    )(held, turned, part, lent, side, from_zhi)
    incoming = lax.all_to_all(outgoing.reshape(4, 448, 128), "col", split_axis=0, concat_axis=0, tiled=True)
    return pl.pallas_call(
        unpack_kernel,
        out_shape=jax.ShapeDtypeStruct((8, 64, 448), BF16),
        in_specs=vmem(1),
        out_specs=pl.BlockSpec(memory_space=pltpu.HBM),
        scratch_shapes=[
            pltpu.VMEM((8, 64, 128), BF16),
            pltpu.VMEM((8, 64, 64), BF16),
            pltpu.SemaphoreType.DMA((4,)),
        ],
        compiler_params=params,
        name="unpack",
    )(incoming.reshape(8, 224, 128))


def solution(mesh):
    in_specs = (
        P("slab", "col", None, None),
        P("slab", "col", None, None),
        P("slab", "col", None, None),
        P(("slab", "col"), None),
    )
    out_specs = P(("slab", "col"), None, None)
    return jax.shard_map(body, mesh=mesh, in_specs=in_specs, out_specs=out_specs, check_vma=False)
```

```python
import jax
import jax.numpy as jnp
from jax import lax
from jax.experimental import pallas as pl
from jax.experimental.pallas import tpu as pltpu
from jax.sharding import PartitionSpec as P

FD = 64
LX = 6
LZ = 2
F32 = jnp.float32
BF16 = jnp.bfloat16


def low_lanes(rows):
    return lax.broadcasted_iota(jnp.int32, (rows, 128), 1) < 64


def even_rows(rows):
    return lax.broadcasted_iota(jnp.int32, (rows, 128), 0) % 2 == 0


def swap_halves(block):
    return jnp.concatenate([block[:, 64:], block[:, :64]], axis=1)


def unpairing():
    row = lax.broadcasted_iota(jnp.int32, (128, 128), 0)
    col = lax.broadcasted_iota(jnp.int32, (128, 128), 1)
    same_y = row // 64 == col % 2
    same_i = row % 64 == (col % 64) // 2 * 2 + col // 64
    return (same_y & same_i).astype(F32).astype(BF16)


def doubled(blocks, matrix):
    low = low_lanes(64)
    stacked = []
    for paired in blocks:
        swapped = swap_halves(paired)
        stacked.append(jnp.concatenate([jnp.where(low, paired, swapped), jnp.where(low, swapped, paired)], axis=0))
    out = jnp.dot(matrix, jnp.concatenate(stacked, axis=1), preferred_element_type=F32).astype(BF16)
    return [out[:, n * 128 : n * 128 + 128] for n in range(len(blocks))]


def diagonal(twice):
    low = low_lanes(64)
    zero = jnp.zeros_like(twice)
    return jnp.concatenate([jnp.where(low, twice, zero), jnp.where(low, zero, twice)], axis=0)


def diagonal_of_packed(packed):
    low = low_lanes(32)
    swapped = swap_halves(packed)
    zero = jnp.zeros_like(packed)
    return jnp.concatenate(
        [
            jnp.where(low, packed, zero),
            jnp.where(low, swapped, zero),
            jnp.where(low, zero, swapped),
            jnp.where(low, zero, packed),
        ],
        axis=0,
    )


def pick_y(both):
    return jnp.where(even_rows(64), both[:, :128], both[:, 128:])


def scales(s_ref, z):
    rows = LX * 64
    row = lax.broadcasted_iota(jnp.int32, (rows, 4 * LX), 0)
    col = lax.broadcasted_iota(jnp.int32, (rows, 4 * LX), 1)
    picks = (col == (row // 64 + z * LX) * 2 + row % 2).astype(F32).astype(BF16)
    spread = jnp.dot(picks, s_ref[...], preferred_element_type=F32)
    row = lax.broadcasted_iota(jnp.int32, (rows, 64), 0)
    col = lax.broadcasted_iota(jnp.int32, (rows, 64), 1)
    spread = jnp.where(row % 64 // 2 == col // 2, spread, 0.0).astype(BF16)
    row = lax.broadcasted_iota(jnp.int32, (64, 128), 0)
    col = lax.broadcasted_iota(jnp.int32, (64, 128), 1)
    halves = (row % 2 == col // 64).astype(F32).astype(BF16)
    return jnp.dot(spread, halves, preferred_element_type=F32)


def smooth_kernel(
    p_hbm, c_hbm, s_hbm, o_hbm, smooth_ref, twice_ref, zlo_ref, zhi_ref, side_ref, c_ref, p_ref, s_ref, o_ref, sems
):
    pairs = range(LZ * LX)
    scaling = pltpu.make_async_copy(s_hbm, s_ref, sems.at[0])
    reading = pltpu.make_async_copy(p_hbm, p_ref, sems.at[1])
    naming = pltpu.make_async_copy(o_hbm, o_ref, sems.at[2])
    first, third, second, last = [
        pltpu.make_async_copy(c_hbm.at[:, lo:hi], c_ref.at[:, lo:hi], sems.at[3 + n])
        for n, (lo, hi) in enumerate(((0, 64), (192, 256), (64, 192), (256, 448)))
    ]
    for copy in (scaling, reading, first, third, naming, second, last):
        copy.start()
    matrix = unpairing()
    even = even_rows(64)
    low = low_lanes(32)
    zero = jnp.zeros((64, 128), BF16)
    scaling.wait()
    scale = [scales(s_ref, z) for z in range(LZ)]
    for copy in (reading, first, third, naming):
        copy.wait()
    tentative = [p_ref[n * 64 : n * 64 + 64, :] for n in pairs]
    twice = doubled(tentative, matrix)
    right = [jnp.concatenate([diagonal(t[:64]), diagonal(t[64:])], axis=1) for t in twice]
    both = [jnp.dot(c_ref[n, 0:64, :], right[n], preferred_element_type=F32) for n in pairs]
    smoothed = [
        (tentative[n].astype(F32) - scale[n // LX][n % LX * 64 : n % LX * 64 + 64] * pick_y(both[n])).astype(BF16)
        for n in pairs
    ]
    left = [transposed_dot(jnp.where(even, c_ref[n, 192:256, :], zero), smoothed[n]) for n in pairs]
    twice = doubled(smoothed, matrix)
    for n in range(0, LZ * LX, 2):
        to = (n + LZ * LX) * 32
        side_ref[to : to + 64, :] = combine(left[n], left[n + 1]).astype(BF16)
    for n in pairs:
        z, x = n // LX, n % LX
        smooth_ref[n * 64 : n * 64 + 64, :] = smoothed[n]
        twice_ref[n] = twice[n]
        for y in range(2):
            packed = jnp.where(low, twice[n][y * 64 : y * 64 + 32], twice[n][y * 64 + 32 : y * 64 + 64])
            to = (x * 2 + y) * 32
            (zlo_ref, zhi_ref)[z][to : to + 32, :] = packed
            if y == 0:
                side_ref[n * 32 : n * 32 + 32, :] = packed
    owners = [jnp.broadcast_to(o_ref[:, a : a + 1], (16, 128)) for a in range(LX // 2)]
    for a in range(LX // 2):
        rank = sum([jnp.where(owners[b] == owners[a], 1, 0) for b in range(a)], jnp.zeros((16, 128), jnp.int32))
        slot = owners[a] * 2 + rank
        to = 2 * LZ * LX * 32 + a * 16
        side_ref[to : to + 16, :] = slot.astype(F32).astype(BF16)
    second.wait()
    last.wait()


def combine(even, odd):
    low = low_lanes(64)
    return jnp.where(low, even[:64], odd[64:]) + swap_halves(jnp.where(low, odd[:64], even[64:]))


def to_low(block):
    return block[:64] + swap_halves(block[64:])


def to_high(block):
    return swap_halves(block[:64]) + block[64:]


def transposed_dot(left, right):
    return lax.dot_general(left, right, (((0,), (0,)), ((), ())), preferred_element_type=F32)


def along_z(z, halo_ref, c_ref, turned, a):
    products = []
    for x in (2 * a, 2 * a + 1):
        right = jnp.concatenate(
            [diagonal_of_packed(halo_ref[(x * 2 + y) * 32 : (x * 2 + y) * 32 + 32, :]) for y in range(2)], axis=1
        )
        block = c_ref[z * LX + x, (5 + z) * 64 : (6 + z) * 64, :]
        products.append(pick_y(jnp.dot(block, right, preferred_element_type=F32)).astype(BF16))
    return to_high(jnp.dot(turned, jnp.concatenate(products, axis=0), preferred_element_type=F32))


def local_kernel(c_ref, smooth_ref, twice_ref, side_ref, zlo_ref, part_ref, lent_ref, turned_ref):
    def both_y(n, swapped=False):
        twice = twice_ref[n]
        first, second = diagonal(twice[:64]), diagonal(twice[64:])
        return jnp.concatenate([second, first] if swapped else [first, second], axis=1)

    even = even_rows(64)
    zero = jnp.zeros((64, 128), BF16)
    inner, outer, across = {}, {}, {}
    for z in range(LZ):
        for x in range(LX):
            n = z * LX + x
            block = lambda d: c_ref[n, d * 64 : d * 64 + 64, :]
            mixed = jnp.where(even, block(4), block(3))
            left = jnp.concatenate([block(0), block(2 - x % 2), block(6 - z), mixed], axis=1)
            right = jnp.concatenate(
                [both_y(n), both_y(z * LX + (x ^ 1)), both_y((1 - z) * LX + x), both_y(n, True)], axis=0
            )
            inner[z, x] = pick_y(jnp.dot(left, right, preferred_element_type=F32)).astype(BF16)
            beside = x - 1 if x % 2 == 0 else x + 1
            if 0 <= beside < LX:
                outer[z, x] = pick_y(
                    jnp.dot(block(1 + x % 2), both_y(z * LX + beside), preferred_element_type=F32)
                ).astype(BF16)
            above = diagonal_of_packed(side_ref[n * 32 : n * 32 + 32, :])
            product = jnp.dot(block(4), above, preferred_element_type=F32).astype(BF16)
            across[z, x] = jnp.where(even, zero, product)
    nothing = jnp.zeros((64, 128), BF16)
    for a in range(LX // 2):
        turned = []
        for z in range(LZ):
            begin = (z * LX + 2 * a) * 64
            turned.append(smooth_ref[begin : begin + 128, :].T)
            turned_ref[a, z] = turned[z]
        right = []
        for z in range(LZ):
            for x in (2 * a, 2 * a + 1):
                beside = outer.get((z, x), nothing)
                ends = [beside, nothing] if x % 2 == 0 else [nothing, beside]
                right.append(jnp.concatenate([inner[z, x], across[z, x]] + ends, axis=1))
        total = jnp.dot(
            jnp.concatenate(turned, axis=1), jnp.concatenate(right, axis=0), preferred_element_type=F32
        )
        part_ref[a, 0:64, :] = combine(total[:, :128], total[:, 256:384]).astype(BF16)
        beyond = along_z(0, zlo_ref, c_ref, turned[0], a)
        part_ref[a, 64:128, :] = jnp.where(low_lanes(64), to_low(total[:, 128:256]), beyond).astype(BF16)
        part_ref[a, 128:192, :] = to_low(total[:, 384:]).astype(BF16)
    low = low_lanes(32)
    lent = [jnp.zeros((32, 128), BF16)] * 8
    for a in range(LX // 2):
        begin = LZ * LX * 32
        left = jnp.concatenate(
            [side_ref[begin + (z * LX + 2 * a) * 32 : begin + (z * LX + 2 * a) * 32 + 64, :] for z in range(LZ)], axis=0
        )
        right = jnp.concatenate(
            [
                jnp.concatenate([twice_ref[z * LX + x, 64:, :] for z in range(LZ)], axis=0)
                for x in (2 * a, 2 * a + 1)
            ],
            axis=1,
        )
        product = transposed_dot(left, right)
        block = product[:64, :128] + product[64:, 128:]
        packed = jnp.where(low, block[:32], block[32:]).astype(BF16)
        slot = side_ref[2 * begin + a * 16 : 2 * begin + a * 16 + 16, :].astype(F32)
        slot = jnp.concatenate([slot, slot], axis=0)
        for place in range(8):
            lent[place] = jnp.where(slot == place, packed.astype(F32), lent[place].astype(F32)).astype(BF16)
    for place in range(8):
        lent_ref[place] = lent[place]


def halo_kernel(c_ref, turned_ref, part_ref, lent_ref, own_ref, zhi_ref, out_ref):
    low = low_lanes(64)
    begin = 2 * LZ * LX * 32
    slots = [own_ref[begin + a * 16 : begin + a * 16 + 16, :].astype(F32) for a in range(LX // 2)]
    here = [[jnp.where(slot == place, 1.0, 0.0).astype(BF16) for slot in slots] for place in range(8)]

    def placed(blocks, place):
        count = blocks[0].shape[0] // 16
        masks = [jnp.concatenate([mask] * count, axis=0) for mask in here[place]]
        return sum([masks[a] * blocks[a] for a in range(1, LX // 2)], masks[0] * blocks[0])

    last = [along_z(1, zhi_ref, c_ref, turned_ref[a, 1], a).astype(BF16) for a in range(LX // 2)]
    ready = [part_ref[a, 0:128, :] for a in range(LX // 2)]
    for place in range(8):
        out_ref[place, 0:128, :] = placed(ready, place)
        out_ref[place, 192:224, :] = lent_ref[place]
    pair = [jnp.where(low, part_ref[a, 128:192, :], last[a]) for a in range(LX // 2)]
    for place in range(8):
        out_ref[place, 128:192, :] = placed(pair, place)


def unpack_kernel(in_ref, out_hbm, middle_ref, last_ref, sems):
    copies = [
        pltpu.make_async_copy(in_ref.at[:, 0:64, :], out_hbm.at[:, :, 0:128], sems.at[0]),
        pltpu.make_async_copy(in_ref.at[:, 64:128, :], out_hbm.at[:, :, 256:384], sems.at[1]),
    ]
    for copy in copies:
        copy.start()
    low = low_lanes(32)
    pairs = [in_ref[slot, 128:192, :] for slot in range(8)]
    for slot in range(8):
        last_ref[slot] = pairs[slot][:, 64:]
    copies.append(pltpu.make_async_copy(last_ref, out_hbm.at[:, :, 384:448], sems.at[2]))
    copies[2].start()
    for slot in range(8):
        lent = in_ref[(slot + 6) % 8, 192:224, :]
        middle_ref[slot, :32, :] = jnp.where(low, pairs[slot][:32], swap_halves(lent))
        middle_ref[slot, 32:, :] = jnp.where(low, pairs[slot][32:], lent)
    copies.append(pltpu.make_async_copy(middle_ref, out_hbm.at[:, :, 128:256], sems.at[3]))
    copies[3].start()
    for copy in copies:
        copy.wait()


def vmem(count):
    return [pl.BlockSpec(memory_space=pltpu.VMEM)] * count


def paired(array):
    layers, across, length, width = array.shape
    lanes = array.transpose(0, 2, 1, 3).reshape(layers, length, across, width // 128, 128)
    return lanes.transpose(0, 1, 3, 2, 4)


def body(prolong, coupling, jacobi_scale, owner):
    tentative = paired(prolong).reshape(LZ * LX * 64, 128)
    blocks = paired(coupling).reshape(LZ * LX, 448, 128)
    scale = jacobi_scale.transpose(0, 2, 1, 3).reshape(LZ * LX * 2, 64)
    names = owner.T
    face = jax.ShapeDtypeStruct((LX * 2 * 32, 128), BF16)
    params = pltpu.CompilerParams(vmem_limit_bytes=40 * 2**20)
    arguments = (tentative, blocks, scale, names)
    smoothed, twice, zlo, zhi, side, held = pl.pallas_call(
        smooth_kernel,
        out_shape=(
            jax.ShapeDtypeStruct((LZ * LX * 64, 128), BF16),
            jax.ShapeDtypeStruct((LZ * LX, 128, 128), BF16),
            face,
            face,
            jax.ShapeDtypeStruct((2 * LZ * LX * 32 + 16 * (LX // 2), 128), BF16),
            jax.ShapeDtypeStruct((LZ * LX, 448, 128), BF16),
        ),
        in_specs=[pl.BlockSpec(memory_space=pltpu.HBM)] * 4,
        out_specs=tuple(vmem(6)),
        scratch_shapes=[
            pltpu.VMEM((LZ * LX * 64, 128), BF16),
            pltpu.VMEM((LZ * LX * 2, 64), BF16),
            pltpu.VMEM((1, LX // 2), jnp.int32),
            pltpu.SemaphoreType.DMA((7,)),
        ],
        compiler_params=params,
        name="smooth",
    )(*(pltpu.with_memory_space_constraint(a, pltpu.HBM) for a in arguments))
    up = lambda a, axis: lax.ppermute(a, axis, [(i, i + 1) for i in range(lax.axis_size(axis) - 1)])
    down = lambda a, axis: lax.ppermute(a, axis, [(i + 1, i) for i in range(lax.axis_size(axis) - 1)])
    from_zlo, from_zhi = up(zhi, "slab"), down(zlo, "slab")
    from_above = down(side, "col")
    part, lent, turned = pl.pallas_call(
        local_kernel,
        out_shape=(
            jax.ShapeDtypeStruct((LX // 2, 192, 128), BF16),
            jax.ShapeDtypeStruct((8, 32, 128), BF16),
            jax.ShapeDtypeStruct((LX // 2, LZ, 128, 128), BF16),
        ),
        in_specs=vmem(5),
        out_specs=tuple(vmem(3)),
        compiler_params=params,
        cost_estimate=pl.CostEstimate(flops=2 * 10**9, bytes_accessed=3 * 10**6, transcendentals=0),
        name="local_blocks",
    )(held, smoothed, twice, from_above, from_zlo)
    outgoing = pl.pallas_call(
        halo_kernel,
        out_shape=jax.ShapeDtypeStruct((8, 224, 128), BF16),
        in_specs=vmem(6),
        out_specs=vmem(1)[0],
        compiler_params=params,
        name="halo_blocks",
    )(held, turned, part, lent, side, from_zhi)
    incoming = lax.all_to_all(outgoing.reshape(4, 448, 128), "col", split_axis=0, concat_axis=0, tiled=True)
    return pl.pallas_call(
        unpack_kernel,
        out_shape=jax.ShapeDtypeStruct((8, 64, 448), BF16),
        in_specs=vmem(1),
        out_specs=pl.BlockSpec(memory_space=pltpu.HBM),
        scratch_shapes=[
            pltpu.VMEM((8, 64, 128), BF16),
            pltpu.VMEM((8, 64, 64), BF16),
            pltpu.SemaphoreType.DMA((4,)),
        ],
        compiler_params=params,
        name="unpack",
    )(incoming.reshape(8, 224, 128))


def solution(mesh):
    in_specs = (
        P("slab", "col", None, None),
        P("slab", "col", None, None),
        P("slab", "col", None, None),
        P(("slab", "col"), None),
    )
    out_specs = P(("slab", "col"), None, None)
    return jax.shard_map(body, mesh=mesh, in_specs=in_specs, out_specs=out_specs, check_vma=False)
```

```python
import jax
import jax.numpy as jnp
from jax import lax
from jax.experimental import pallas as pl
from jax.experimental.pallas import tpu as pltpu
from jax.sharding import PartitionSpec as P

FD = 64
LX = 6
LZ = 2
F32 = jnp.float32
BF16 = jnp.bfloat16


def low_lanes(rows):
    return lax.broadcasted_iota(jnp.int32, (rows, 128), 1) < 64


def even_rows(rows):
    return lax.broadcasted_iota(jnp.int32, (rows, 128), 0) % 2 == 0


def swap_halves(block):
    return jnp.concatenate([block[:, 64:], block[:, :64]], axis=1)


def unpairing():
    row = lax.broadcasted_iota(jnp.int32, (128, 128), 0)
    col = lax.broadcasted_iota(jnp.int32, (128, 128), 1)
    same_y = row // 64 == col % 2
    same_i = row % 64 == (col % 64) // 2 * 2 + col // 64
    return (same_y & same_i).astype(F32).astype(BF16)


def doubled(blocks, matrix):
    low = low_lanes(64)
    stacked = []
    for paired in blocks:
        swapped = swap_halves(paired)
        stacked.append(jnp.concatenate([jnp.where(low, paired, swapped), jnp.where(low, swapped, paired)], axis=0))
    out = jnp.dot(matrix, jnp.concatenate(stacked, axis=1), preferred_element_type=F32).astype(BF16)
    return [out[:, n * 128 : n * 128 + 128] for n in range(len(blocks))]


def diagonal(twice):
    low = low_lanes(64)
    zero = jnp.zeros_like(twice)
    return jnp.concatenate([jnp.where(low, twice, zero), jnp.where(low, zero, twice)], axis=0)


def diagonal_of_packed(packed):
    low = low_lanes(32)
    swapped = swap_halves(packed)
    zero = jnp.zeros_like(packed)
    return jnp.concatenate(
        [
            jnp.where(low, packed, zero),
            jnp.where(low, swapped, zero),
            jnp.where(low, zero, swapped),
            jnp.where(low, zero, packed),
        ],
        axis=0,
    )


def pick_y(both):
    return jnp.where(even_rows(64), both[:, :128], both[:, 128:])


def scales(s_ref, z):
    rows = LX * 64
    row = lax.broadcasted_iota(jnp.int32, (rows, 4 * LX), 0)
    col = lax.broadcasted_iota(jnp.int32, (rows, 4 * LX), 1)
    picks = (col == (row // 64 + z * LX) * 2 + row % 2).astype(F32).astype(BF16)
    spread = jnp.dot(picks, s_ref[...], preferred_element_type=F32)
    row = lax.broadcasted_iota(jnp.int32, (rows, 64), 0)
    col = lax.broadcasted_iota(jnp.int32, (rows, 64), 1)
    spread = jnp.where(row % 64 // 2 == col // 2, spread, 0.0).astype(BF16)
    row = lax.broadcasted_iota(jnp.int32, (64, 128), 0)
    col = lax.broadcasted_iota(jnp.int32, (64, 128), 1)
    halves = (row % 2 == col // 64).astype(F32).astype(BF16)
    return jnp.dot(spread, halves, preferred_element_type=F32)


def smooth_kernel(
    p_hbm, c_hbm, s_hbm, o_hbm, smooth_ref, twice_ref, zlo_ref, zhi_ref, side_ref, c_ref, p_ref, s_ref, o_ref, sems
):
    pairs = range(LZ * LX)
    scaling = pltpu.make_async_copy(s_hbm, s_ref, sems.at[0])
    reading = pltpu.make_async_copy(p_hbm, p_ref, sems.at[1])
    naming = pltpu.make_async_copy(o_hbm, o_ref, sems.at[2])
    first, third, second, last = [
        pltpu.make_async_copy(c_hbm.at[:, lo:hi], c_ref.at[:, lo:hi], sems.at[3 + n])
        for n, (lo, hi) in enumerate(((0, 64), (192, 256), (64, 192), (256, 448)))
    ]
    for copy in (scaling, reading, first, third, naming, second, last):
        copy.start()
    matrix = unpairing()
    even = even_rows(64)
    low = low_lanes(32)
    zero = jnp.zeros((64, 128), BF16)
    scaling.wait()
    scale = [scales(s_ref, z) for z in range(LZ)]
    for copy in (reading, first, third, naming):
        copy.wait()
    tentative = [p_ref[n * 64 : n * 64 + 64, :] for n in pairs]
    twice = doubled(tentative, matrix)
    right = [jnp.concatenate([diagonal(t[:64]), diagonal(t[64:])], axis=1) for t in twice]
    both = [jnp.dot(c_ref[n, 0:64, :], right[n], preferred_element_type=F32) for n in pairs]
    smoothed = [
        (tentative[n].astype(F32) - scale[n // LX][n % LX * 64 : n % LX * 64 + 64] * pick_y(both[n])).astype(BF16)
        for n in pairs
    ]
    left = [transposed_dot(jnp.where(even, c_ref[n, 192:256, :], zero), smoothed[n]) for n in pairs]
    twice = doubled(smoothed, matrix)
    for n in range(0, LZ * LX, 2):
        to = (n + LZ * LX) * 32
        side_ref[to : to + 64, :] = combine(left[n], left[n + 1]).astype(BF16)
    for n in pairs:
        z, x = n // LX, n % LX
        smooth_ref[n * 64 : n * 64 + 64, :] = smoothed[n]
        twice_ref[n] = twice[n]
        for y in range(2):
            packed = jnp.where(low, twice[n][y * 64 : y * 64 + 32], twice[n][y * 64 + 32 : y * 64 + 64])
            to = (x * 2 + y) * 32
            (zlo_ref, zhi_ref)[z][to : to + 32, :] = packed
            if y == 0:
                side_ref[n * 32 : n * 32 + 32, :] = packed
    owners = [jnp.broadcast_to(o_ref[:, a : a + 1], (16, 128)) for a in range(LX // 2)]
    for a in range(LX // 2):
        rank = sum([jnp.where(owners[b] == owners[a], 1, 0) for b in range(a)], jnp.zeros((16, 128), jnp.int32))
        slot = owners[a] * 2 + rank
        to = 2 * LZ * LX * 32 + a * 16
        side_ref[to : to + 16, :] = slot.astype(F32).astype(BF16)
    second.wait()
    last.wait()


def combine(even, odd):
    low = low_lanes(64)
    return jnp.where(low, even[:64], odd[64:]) + swap_halves(jnp.where(low, odd[:64], even[64:]))


def to_low(block):
    return block[:64] + swap_halves(block[64:])


def to_high(block):
    return swap_halves(block[:64]) + block[64:]


def transposed_dot(left, right):
    return lax.dot_general(left, right, (((0,), (0,)), ((), ())), preferred_element_type=F32)


def along_z(z, halo_ref, c_ref, turned, a):
    products = []
    for x in (2 * a, 2 * a + 1):
        right = jnp.concatenate(
            [diagonal_of_packed(halo_ref[(x * 2 + y) * 32 : (x * 2 + y) * 32 + 32, :]) for y in range(2)], axis=1
        )
        block = c_ref[z * LX + x, (5 + z) * 64 : (6 + z) * 64, :]
        products.append(pick_y(jnp.dot(block, right, preferred_element_type=F32)).astype(BF16))
    return to_high(jnp.dot(turned, jnp.concatenate(products, axis=0), preferred_element_type=F32))


def places(own_ref):
    begin = 2 * LZ * LX * 32
    slots = [own_ref[begin + a * 16 : begin + a * 16 + 16, :].astype(F32) for a in range(LX // 2)]
    return [[jnp.where(slot == place, 1.0, 0.0).astype(BF16) for slot in slots] for place in range(8)]


def placed(blocks, here):
    masks = [jnp.concatenate([mask] * (blocks[0].shape[0] // 16), axis=0) for mask in here]
    return sum([masks[a] * blocks[a] for a in range(1, LX // 2)], masks[0] * blocks[0])


def local_kernel(c_ref, smooth_ref, twice_ref, side_ref, zlo_ref, own_ref, out_ref, part_ref, turned_ref):
    def both_y(n, swapped=False):
        twice = twice_ref[n]
        first, second = diagonal(twice[:64]), diagonal(twice[64:])
        return jnp.concatenate([second, first] if swapped else [first, second], axis=1)

    even = even_rows(64)
    zero = jnp.zeros((64, 128), BF16)
    inner, outer, across = {}, {}, {}
    for z in range(LZ):
        for x in range(LX):
            n = z * LX + x
            block = lambda d: c_ref[n, d * 64 : d * 64 + 64, :]
            mixed = jnp.where(even, block(4), block(3))
            left = jnp.concatenate([block(0), block(2 - x % 2), block(6 - z), mixed], axis=1)
            right = jnp.concatenate(
                [both_y(n), both_y(z * LX + (x ^ 1)), both_y((1 - z) * LX + x), both_y(n, True)], axis=0
            )
            inner[z, x] = pick_y(jnp.dot(left, right, preferred_element_type=F32)).astype(BF16)
            beside = x - 1 if x % 2 == 0 else x + 1
            if 0 <= beside < LX:
                outer[z, x] = pick_y(
                    jnp.dot(block(1 + x % 2), both_y(z * LX + beside), preferred_element_type=F32)
                ).astype(BF16)
            above = diagonal_of_packed(side_ref[n * 32 : n * 32 + 32, :])
            product = jnp.dot(block(4), above, preferred_element_type=F32).astype(BF16)
            across[z, x] = jnp.where(even, zero, product)
    nothing = jnp.zeros((64, 128), BF16)
    ready = []
    for a in range(LX // 2):
        turned = []
        for z in range(LZ):
            begin = (z * LX + 2 * a) * 64
            turned.append(smooth_ref[begin : begin + 128, :].T)
            turned_ref[a, z] = turned[z]
        right = []
        for z in range(LZ):
            for x in (2 * a, 2 * a + 1):
                beside = outer.get((z, x), nothing)
                ends = [beside, nothing] if x % 2 == 0 else [nothing, beside]
                right.append(jnp.concatenate([inner[z, x], across[z, x]] + ends, axis=1))
        total = jnp.dot(
            jnp.concatenate(turned, axis=1), jnp.concatenate(right, axis=0), preferred_element_type=F32
        )
        first = combine(total[:, :128], total[:, 256:384]).astype(BF16)
        beyond = along_z(0, zlo_ref, c_ref, turned[0], a)
        second = jnp.where(low_lanes(64), to_low(total[:, 128:256]), beyond).astype(BF16)
        ready.append(jnp.concatenate([first, second], axis=0))
        part_ref[a] = to_low(total[:, 384:]).astype(BF16)
    here = places(own_ref)
    for place in range(8):
        out_ref[place, 0:128, :] = placed(ready, here[place])
    low = low_lanes(32)
    lent = [jnp.zeros((32, 128), BF16)] * 8
    for a in range(LX // 2):
        begin = LZ * LX * 32
        left = jnp.concatenate(
            [side_ref[begin + (z * LX + 2 * a) * 32 : begin + (z * LX + 2 * a) * 32 + 64, :] for z in range(LZ)], axis=0
        )
        right = jnp.concatenate(
            [
                jnp.concatenate([twice_ref[z * LX + x, 64:, :] for z in range(LZ)], axis=0)
                for x in (2 * a, 2 * a + 1)
            ],
            axis=1,
        )
        product = transposed_dot(left, right)
        block = product[:64, :128] + product[64:, 128:]
        packed = jnp.where(low, block[:32], block[32:]).astype(BF16)
        slot = side_ref[2 * begin + a * 16 : 2 * begin + a * 16 + 16, :].astype(F32)
        slot = jnp.concatenate([slot, slot], axis=0)
        for place in range(8):
            lent[place] = jnp.where(slot == place, packed.astype(F32), lent[place].astype(F32)).astype(BF16)
    for place in range(8):
        out_ref[place, 192:224, :] = lent[place]


def halo_kernel(c_ref, turned_ref, part_ref, outgoing_ref, own_ref, zhi_ref, out_ref):
    low = low_lanes(64)
    here = places(own_ref)
    last = [along_z(1, zhi_ref, c_ref, turned_ref[a, 1], a).astype(BF16) for a in range(LX // 2)]
    pair = [jnp.where(low, part_ref[a], last[a]) for a in range(LX // 2)]
    for place in range(8):
        out_ref[place, 128:192, :] = placed(pair, here[place])


def unpack_kernel(in_ref, out_hbm, middle_ref, last_ref, sems):
    copies = [
        pltpu.make_async_copy(in_ref.at[:, 0:64, :], out_hbm.at[:, :, 0:128], sems.at[0]),
        pltpu.make_async_copy(in_ref.at[:, 64:128, :], out_hbm.at[:, :, 256:384], sems.at[1]),
    ]
    for copy in copies:
        copy.start()
    low = low_lanes(32)
    pairs = [in_ref[slot, 128:192, :] for slot in range(8)]
    for slot in range(8):
        last_ref[slot] = pairs[slot][:, 64:]
    copies.append(pltpu.make_async_copy(last_ref, out_hbm.at[:, :, 384:448], sems.at[2]))
    copies[2].start()
    for slot in range(8):
        lent = in_ref[(slot + 6) % 8, 192:224, :]
        middle_ref[slot, :32, :] = jnp.where(low, pairs[slot][:32], swap_halves(lent))
        middle_ref[slot, 32:, :] = jnp.where(low, pairs[slot][32:], lent)
    copies.append(pltpu.make_async_copy(middle_ref, out_hbm.at[:, :, 128:256], sems.at[3]))
    copies[3].start()
    for copy in copies:
        copy.wait()


def vmem(count):
    return [pl.BlockSpec(memory_space=pltpu.VMEM)] * count


def paired(array):
    layers, across, length, width = array.shape
    lanes = array.transpose(0, 2, 1, 3).reshape(layers, length, across, width // 128, 128)
    return lanes.transpose(0, 1, 3, 2, 4)


def body(prolong, coupling, jacobi_scale, owner):
    tentative = paired(prolong).reshape(LZ * LX * 64, 128)
    blocks = paired(coupling).reshape(LZ * LX, 448, 128)
    scale = jacobi_scale.transpose(0, 2, 1, 3).reshape(LZ * LX * 2, 64)
    names = owner.T
    face = jax.ShapeDtypeStruct((LX * 2 * 32, 128), BF16)
    params = pltpu.CompilerParams(vmem_limit_bytes=40 * 2**20)
    arguments = (tentative, blocks, scale, names)
    smoothed, twice, zlo, zhi, side, held = pl.pallas_call(
        smooth_kernel,
        out_shape=(
            jax.ShapeDtypeStruct((LZ * LX * 64, 128), BF16),
            jax.ShapeDtypeStruct((LZ * LX, 128, 128), BF16),
            face,
            face,
            jax.ShapeDtypeStruct((2 * LZ * LX * 32 + 16 * (LX // 2), 128), BF16),
            jax.ShapeDtypeStruct((LZ * LX, 448, 128), BF16),
        ),
        in_specs=[pl.BlockSpec(memory_space=pltpu.HBM)] * 4,
        out_specs=tuple(vmem(6)),
        scratch_shapes=[
            pltpu.VMEM((LZ * LX * 64, 128), BF16),
            pltpu.VMEM((LZ * LX * 2, 64), BF16),
            pltpu.VMEM((1, LX // 2), jnp.int32),
            pltpu.SemaphoreType.DMA((7,)),
        ],
        compiler_params=params,
        name="smooth",
    )(*(pltpu.with_memory_space_constraint(a, pltpu.HBM) for a in arguments))
    up = lambda a, axis: lax.ppermute(a, axis, [(i, i + 1) for i in range(lax.axis_size(axis) - 1)])
    down = lambda a, axis: lax.ppermute(a, axis, [(i + 1, i) for i in range(lax.axis_size(axis) - 1)])
    from_zlo, from_zhi = up(zhi, "slab"), down(zlo, "slab")
    from_above = down(side, "col")
    partial, part, turned = pl.pallas_call(
        local_kernel,
        out_shape=(
            jax.ShapeDtypeStruct((8, 224, 128), BF16),
            jax.ShapeDtypeStruct((LX // 2, 64, 128), BF16),
            jax.ShapeDtypeStruct((LX // 2, LZ, 128, 128), BF16),
        ),
        in_specs=vmem(6),
        out_specs=tuple(vmem(3)),
        compiler_params=params,
        cost_estimate=pl.CostEstimate(flops=2 * 10**9, bytes_accessed=3 * 10**6, transcendentals=0),
        name="local_blocks",
    )(held, smoothed, twice, from_above, from_zlo, side)
    outgoing = pl.pallas_call(
        halo_kernel,
        out_shape=jax.ShapeDtypeStruct((8, 224, 128), BF16),
        in_specs=vmem(6),
        out_specs=vmem(1)[0],
        input_output_aliases={3: 0},
        compiler_params=params,
        name="halo_blocks",
    )(held, turned, part, partial, side, from_zhi)
    incoming = lax.all_to_all(outgoing.reshape(4, 448, 128), "col", split_axis=0, concat_axis=0, tiled=True)
    return pl.pallas_call(
        unpack_kernel,
        out_shape=jax.ShapeDtypeStruct((8, 64, 448), BF16),
        in_specs=vmem(1),
        out_specs=pl.BlockSpec(memory_space=pltpu.HBM),
        scratch_shapes=[
            pltpu.VMEM((8, 64, 128), BF16),
            pltpu.VMEM((8, 64, 64), BF16),
            pltpu.SemaphoreType.DMA((4,)),
        ],
        compiler_params=params,
        name="unpack",
    )(incoming.reshape(8, 224, 128))


def solution(mesh):
    in_specs = (
        P("slab", "col", None, None),
        P("slab", "col", None, None),
        P("slab", "col", None, None),
        P(("slab", "col"), None),
    )
    out_specs = P(("slab", "col"), None, None)
    return jax.shard_map(body, mesh=mesh, in_specs=in_specs, out_specs=out_specs, check_vma=False)
```

```python
import jax
import jax.numpy as jnp
from jax import lax
from jax.experimental import pallas as pl
from jax.experimental.pallas import tpu as pltpu
from jax.sharding import PartitionSpec as P

FD = 64
LX = 6
LZ = 2
F32 = jnp.float32
BF16 = jnp.bfloat16


def low_lanes(rows):
    return lax.broadcasted_iota(jnp.int32, (rows, 128), 1) < 64


def even_rows(rows):
    return lax.broadcasted_iota(jnp.int32, (rows, 128), 0) % 2 == 0


def swap_halves(block):
    return jnp.concatenate([block[:, 64:], block[:, :64]], axis=1)


def unpairing():
    row = lax.broadcasted_iota(jnp.int32, (128, 128), 0)
    col = lax.broadcasted_iota(jnp.int32, (128, 128), 1)
    same_y = row // 64 == col % 2
    same_i = row % 64 == (col % 64) // 2 * 2 + col // 64
    return (same_y & same_i).astype(F32).astype(BF16)


def doubled(blocks, matrix):
    low = low_lanes(64)
    stacked = []
    for paired in blocks:
        swapped = swap_halves(paired)
        stacked.append(jnp.concatenate([jnp.where(low, paired, swapped), jnp.where(low, swapped, paired)], axis=0))
    out = jnp.dot(matrix, jnp.concatenate(stacked, axis=1), preferred_element_type=F32).astype(BF16)
    return [out[:, n * 128 : n * 128 + 128] for n in range(len(blocks))]


def diagonal(twice):
    low = low_lanes(64)
    zero = jnp.zeros_like(twice)
    return jnp.concatenate([jnp.where(low, twice, zero), jnp.where(low, zero, twice)], axis=0)


def diagonal_of_packed(packed):
    low = low_lanes(32)
    swapped = swap_halves(packed)
    zero = jnp.zeros_like(packed)
    return jnp.concatenate(
        [
            jnp.where(low, packed, zero),
            jnp.where(low, swapped, zero),
            jnp.where(low, zero, swapped),
            jnp.where(low, zero, packed),
        ],
        axis=0,
    )


def pick_y(both):
    return jnp.where(even_rows(64), both[:, :128], both[:, 128:])


def scales(s_ref, z):
    rows = LX * 64
    row = lax.broadcasted_iota(jnp.int32, (rows, 4 * LX), 0)
    col = lax.broadcasted_iota(jnp.int32, (rows, 4 * LX), 1)
    picks = (col == (row // 64 + z * LX) * 2 + row % 2).astype(F32).astype(BF16)
    spread = jnp.dot(picks, s_ref[...], preferred_element_type=F32)
    row = lax.broadcasted_iota(jnp.int32, (rows, 64), 0)
    col = lax.broadcasted_iota(jnp.int32, (rows, 64), 1)
    spread = jnp.where(row % 64 // 2 == col // 2, spread, 0.0).astype(BF16)
    row = lax.broadcasted_iota(jnp.int32, (64, 128), 0)
    col = lax.broadcasted_iota(jnp.int32, (64, 128), 1)
    halves = (row % 2 == col // 64).astype(F32).astype(BF16)
    return jnp.dot(spread, halves, preferred_element_type=F32)


def smooth_kernel(
    p_hbm, c_hbm, s_hbm, o_hbm, smooth_ref, twice_ref, zlo_ref, zhi_ref, side_ref, c_ref, p_ref, s_ref, o_ref, sems
):
    pairs = range(LZ * LX)
    scaling = pltpu.make_async_copy(s_hbm, s_ref, sems.at[0])
    reading = pltpu.make_async_copy(p_hbm, p_ref, sems.at[1])
    naming = pltpu.make_async_copy(o_hbm, o_ref, sems.at[2])
    first, third, second, last = [
        pltpu.make_async_copy(c_hbm.at[:, lo:hi], c_ref.at[:, lo:hi], sems.at[3 + n])
        for n, (lo, hi) in enumerate(((0, 64), (192, 256), (64, 192), (256, 448)))
    ]
    for copy in (scaling, reading, first, third, naming, second, last):
        copy.start()
    matrix = unpairing()
    even = even_rows(64)
    low = low_lanes(32)
    zero = jnp.zeros((64, 128), BF16)
    scaling.wait()
    scale = [scales(s_ref, z) for z in range(LZ)]
    for copy in (reading, first, third, naming):
        copy.wait()
    tentative = [p_ref[n * 64 : n * 64 + 64, :] for n in pairs]
    twice = doubled(tentative, matrix)
    right = [jnp.concatenate([diagonal(t[:64]), diagonal(t[64:])], axis=1) for t in twice]
    both = [jnp.dot(c_ref[n, 0:64, :], right[n], preferred_element_type=F32) for n in pairs]
    smoothed = [
        (tentative[n].astype(F32) - scale[n // LX][n % LX * 64 : n % LX * 64 + 64] * pick_y(both[n])).astype(BF16)
        for n in pairs
    ]
    left = [transposed_dot(jnp.where(even, c_ref[n, 192:256, :], zero), smoothed[n]) for n in pairs]
    twice = doubled(smoothed, matrix)
    for n in range(0, LZ * LX, 2):
        to = (n + LZ * LX) * 32
        side_ref[to : to + 64, :] = combine(left[n], left[n + 1]).astype(BF16)
    for n in pairs:
        z, x = n // LX, n % LX
        smooth_ref[n * 64 : n * 64 + 64, :] = smoothed[n]
        twice_ref[n] = twice[n]
        for y in range(2):
            packed = jnp.where(low, twice[n][y * 64 : y * 64 + 32], twice[n][y * 64 + 32 : y * 64 + 64])
            to = (x * 2 + y) * 32
            (zlo_ref, zhi_ref)[z][to : to + 32, :] = packed
            if y == 0:
                side_ref[n * 32 : n * 32 + 32, :] = packed
    owners = [jnp.broadcast_to(o_ref[:, a : a + 1], (16, 128)) for a in range(LX // 2)]
    for a in range(LX // 2):
        rank = sum([jnp.where(owners[b] == owners[a], 1, 0) for b in range(a)], jnp.zeros((16, 128), jnp.int32))
        slot = owners[a] * 2 + rank
        to = 2 * LZ * LX * 32 + a * 16
        side_ref[to : to + 16, :] = slot.astype(F32).astype(BF16)
    second.wait()
    last.wait()


def combine(even, odd):
    low = low_lanes(64)
    return jnp.where(low, even[:64], odd[64:]) + swap_halves(jnp.where(low, odd[:64], even[64:]))


def to_low(block):
    return block[:64] + swap_halves(block[64:])


def to_high(block):
    return swap_halves(block[:64]) + block[64:]


def transposed_dot(left, right):
    return lax.dot_general(left, right, (((0,), (0,)), ((), ())), preferred_element_type=F32)


def along_z(z, halo_ref, c_ref, turned, a):
    products = []
    even = even_rows(64)
    for x in (2 * a, 2 * a + 1):
        right = jnp.concatenate(
            [diagonal_of_packed(halo_ref[(x * 2 + y) * 32 : (x * 2 + y) * 32 + 32, :]) for y in range(2)], axis=0
        )
        block = c_ref[z * LX + x, (5 + z) * 64 : (6 + z) * 64, :]
        zero = jnp.zeros_like(block)
        left = jnp.concatenate([jnp.where(even, block, zero), jnp.where(even, zero, block)], axis=1)
        products.append(jnp.dot(left, right, preferred_element_type=F32).astype(BF16))
    return to_high(jnp.dot(turned, jnp.concatenate(products, axis=0), preferred_element_type=F32))


def local_kernel(c_ref, smooth_ref, twice_ref, side_ref, zlo_ref, part_ref, lent_ref, turned_ref):
    def both_y(n, swapped=False):
        twice = twice_ref[n]
        first, second = diagonal(twice[:64]), diagonal(twice[64:])
        return jnp.concatenate([second, first] if swapped else [first, second], axis=1)

    even = even_rows(64)
    zero = jnp.zeros((64, 128), BF16)
    inner, outer, across = {}, {}, {}
    for z in range(LZ):
        for x in range(LX):
            n = z * LX + x
            block = lambda d: c_ref[n, d * 64 : d * 64 + 64, :]
            mixed = jnp.where(even, block(4), block(3))
            left = jnp.concatenate([block(0), block(2 - x % 2), block(6 - z), mixed], axis=1)
            right = jnp.concatenate(
                [both_y(n), both_y(z * LX + (x ^ 1)), both_y((1 - z) * LX + x), both_y(n, True)], axis=0
            )
            inner[z, x] = pick_y(jnp.dot(left, right, preferred_element_type=F32)).astype(BF16)
            beside = x - 1 if x % 2 == 0 else x + 1
            if 0 <= beside < LX:
                outer[z, x] = pick_y(
                    jnp.dot(block(1 + x % 2), both_y(z * LX + beside), preferred_element_type=F32)
                ).astype(BF16)
            above = diagonal_of_packed(side_ref[n * 32 : n * 32 + 32, :])
            product = jnp.dot(block(4), above, preferred_element_type=F32).astype(BF16)
            across[z, x] = jnp.where(even, zero, product)
    nothing = jnp.zeros((64, 128), BF16)
    for a in range(LX // 2):
        turned = []
        for z in range(LZ):
            begin = (z * LX + 2 * a) * 64
            turned.append(smooth_ref[begin : begin + 128, :].T)
            turned_ref[a, z] = turned[z]
        right = []
        for z in range(LZ):
            for x in (2 * a, 2 * a + 1):
                beside = outer.get((z, x), nothing)
                ends = [beside, nothing] if x % 2 == 0 else [nothing, beside]
                right.append(jnp.concatenate([inner[z, x], across[z, x]] + ends, axis=1))
        total = jnp.dot(
            jnp.concatenate(turned, axis=1), jnp.concatenate(right, axis=0), preferred_element_type=F32
        )
        part_ref[a, 0:64, :] = combine(total[:, :128], total[:, 256:384]).astype(BF16)
        beyond = along_z(0, zlo_ref, c_ref, turned[0], a)
        part_ref[a, 64:128, :] = jnp.where(low_lanes(64), to_low(total[:, 128:256]), beyond).astype(BF16)
        part_ref[a, 128:192, :] = to_low(total[:, 384:]).astype(BF16)
    low = low_lanes(32)
    lent = [jnp.zeros((32, 128), BF16)] * 8
    for a in range(LX // 2):
        begin = LZ * LX * 32
        left = jnp.concatenate(
            [side_ref[begin + (z * LX + 2 * a) * 32 : begin + (z * LX + 2 * a) * 32 + 64, :] for z in range(LZ)], axis=0
        )
        right = jnp.concatenate(
            [
                jnp.concatenate([twice_ref[z * LX + x, 64:, :] for z in range(LZ)], axis=0)
                for x in (2 * a, 2 * a + 1)
            ],
            axis=1,
        )
        product = transposed_dot(left, right)
        block = product[:64, :128] + product[64:, 128:]
        packed = jnp.where(low, block[:32], block[32:]).astype(BF16)
        slot = side_ref[2 * begin + a * 16 : 2 * begin + a * 16 + 16, :].astype(F32)
        slot = jnp.concatenate([slot, slot], axis=0)
        for place in range(8):
            lent[place] = jnp.where(slot == place, packed.astype(F32), lent[place].astype(F32)).astype(BF16)
    for place in range(8):
        lent_ref[place] = lent[place]


def halo_kernel(c_ref, turned_ref, part_ref, lent_ref, own_ref, zhi_ref, out_ref):
    low = low_lanes(64)
    begin = 2 * LZ * LX * 32
    slots = [own_ref[begin + a * 16 : begin + a * 16 + 16, :].astype(F32) for a in range(LX // 2)]
    here = [[jnp.where(slot == place, 1.0, 0.0).astype(BF16) for slot in slots] for place in range(8)]

    def placed(blocks, place):
        count = blocks[0].shape[0] // 16
        masks = [jnp.concatenate([mask] * count, axis=0) for mask in here[place]]
        return sum([masks[a] * blocks[a] for a in range(1, LX // 2)], masks[0] * blocks[0])

    last = [along_z(1, zhi_ref, c_ref, turned_ref[a, 1], a).astype(BF16) for a in range(LX // 2)]
    ready = [part_ref[a, 0:128, :] for a in range(LX // 2)]
    for place in range(8):
        out_ref[place, 0:128, :] = placed(ready, place)
        out_ref[place, 192:224, :] = lent_ref[place]
    pair = [jnp.where(low, part_ref[a, 128:192, :], last[a]) for a in range(LX // 2)]
    for place in range(8):
        out_ref[place, 128:192, :] = placed(pair, place)


def unpack_kernel(in_ref, out_hbm, middle_ref, last_ref, sems):
    copies = [
        pltpu.make_async_copy(in_ref.at[:, 0:64, :], out_hbm.at[:, :, 0:128], sems.at[0]),
        pltpu.make_async_copy(in_ref.at[:, 64:128, :], out_hbm.at[:, :, 256:384], sems.at[1]),
    ]
    for copy in copies:
        copy.start()
    low = low_lanes(32)
    pairs = [in_ref[slot, 128:192, :] for slot in range(8)]
    for slot in range(8):
        last_ref[slot] = pairs[slot][:, 64:]
    copies.append(pltpu.make_async_copy(last_ref, out_hbm.at[:, :, 384:448], sems.at[2]))
    copies[2].start()
    for slot in range(8):
        lent = in_ref[(slot + 6) % 8, 192:224, :]
        middle_ref[slot, :32, :] = jnp.where(low, pairs[slot][:32], swap_halves(lent))
        middle_ref[slot, 32:, :] = jnp.where(low, pairs[slot][32:], lent)
    copies.append(pltpu.make_async_copy(middle_ref, out_hbm.at[:, :, 128:256], sems.at[3]))
    copies[3].start()
    for copy in copies:
        copy.wait()


def vmem(count):
    return [pl.BlockSpec(memory_space=pltpu.VMEM)] * count


def paired(array):
    layers, across, length, width = array.shape
    lanes = array.transpose(0, 2, 1, 3).reshape(layers, length, across, width // 128, 128)
    return lanes.transpose(0, 1, 3, 2, 4)


def body(prolong, coupling, jacobi_scale, owner):
    tentative = paired(prolong).reshape(LZ * LX * 64, 128)
    blocks = paired(coupling).reshape(LZ * LX, 448, 128)
    scale = jacobi_scale.transpose(0, 2, 1, 3).reshape(LZ * LX * 2, 64)
    names = owner.T
    face = jax.ShapeDtypeStruct((LX * 2 * 32, 128), BF16)
    params = pltpu.CompilerParams(vmem_limit_bytes=40 * 2**20)
    arguments = (tentative, blocks, scale, names)
    smoothed, twice, zlo, zhi, side, held = pl.pallas_call(
        smooth_kernel,
        out_shape=(
            jax.ShapeDtypeStruct((LZ * LX * 64, 128), BF16),
            jax.ShapeDtypeStruct((LZ * LX, 128, 128), BF16),
            face,
            face,
            jax.ShapeDtypeStruct((2 * LZ * LX * 32 + 16 * (LX // 2), 128), BF16),
            jax.ShapeDtypeStruct((LZ * LX, 448, 128), BF16),
        ),
        in_specs=[pl.BlockSpec(memory_space=pltpu.HBM)] * 4,
        out_specs=tuple(vmem(6)),
        scratch_shapes=[
            pltpu.VMEM((LZ * LX * 64, 128), BF16),
            pltpu.VMEM((LZ * LX * 2, 64), BF16),
            pltpu.VMEM((1, LX // 2), jnp.int32),
            pltpu.SemaphoreType.DMA((7,)),
        ],
        compiler_params=params,
        name="smooth",
    )(*(pltpu.with_memory_space_constraint(a, pltpu.HBM) for a in arguments))
    up = lambda a, axis: lax.ppermute(a, axis, [(i, i + 1) for i in range(lax.axis_size(axis) - 1)])
    down = lambda a, axis: lax.ppermute(a, axis, [(i + 1, i) for i in range(lax.axis_size(axis) - 1)])
    from_zlo, from_zhi = up(zhi, "slab"), down(zlo, "slab")
    from_above = down(side, "col")
    part, lent, turned = pl.pallas_call(
        local_kernel,
        out_shape=(
            jax.ShapeDtypeStruct((LX // 2, 192, 128), BF16),
            jax.ShapeDtypeStruct((8, 32, 128), BF16),
            jax.ShapeDtypeStruct((LX // 2, LZ, 128, 128), BF16),
        ),
        in_specs=vmem(5),
        out_specs=tuple(vmem(3)),
        compiler_params=params,
        cost_estimate=pl.CostEstimate(flops=2 * 10**9, bytes_accessed=3 * 10**6, transcendentals=0),
        name="local_blocks",
    )(held, smoothed, twice, from_above, from_zlo)
    outgoing = pl.pallas_call(
        halo_kernel,
        out_shape=jax.ShapeDtypeStruct((8, 224, 128), BF16),
        in_specs=vmem(6),
        out_specs=vmem(1)[0],
        compiler_params=params,
        name="halo_blocks",
    )(held, turned, part, lent, side, from_zhi)
    incoming = lax.all_to_all(outgoing.reshape(4, 448, 128), "col", split_axis=0, concat_axis=0, tiled=True)
    return pl.pallas_call(
        unpack_kernel,
        out_shape=jax.ShapeDtypeStruct((8, 64, 448), BF16),
        in_specs=vmem(1),
        out_specs=pl.BlockSpec(memory_space=pltpu.HBM),
        scratch_shapes=[
            pltpu.VMEM((8, 64, 128), BF16),
            pltpu.VMEM((8, 64, 64), BF16),
            pltpu.SemaphoreType.DMA((4,)),
        ],
        compiler_params=params,
        name="unpack",
    )(incoming.reshape(8, 224, 128))


def solution(mesh):
    in_specs = (
        P("slab", "col", None, None),
        P("slab", "col", None, None),
        P("slab", "col", None, None),
        P(("slab", "col"), None),
    )
    out_specs = P(("slab", "col"), None, None)
    return jax.shard_map(body, mesh=mesh, in_specs=in_specs, out_specs=out_specs, check_vma=False)
```
